512 devices in a mesh: group: 8 (over y, core), loop: 16 (over x, z_hi), mp: 4 (over z_lo).
Axes of the slice: x: 4, y: 4, z: 16 (z_hi: 4, z_lo: 4; z = z_hi * 4 + z_lo), core: 2. Of those that a mesh axis runs over, the one named last changes fastest.
Arguments:
- hidden_in: bfloat16 [16384, 8192], P(('group', 'loop'), 'mp'), may hold values from -11 to 11
- norm_gain: float32 [8192], P('mp'), may hold values from 0.5 to 1.5
- key_cotangent: bfloat16 [16384, 1024], P(('group', 'loop'), 'mp'), may hold values from -0.046875 to 0.046875
- value_cotangent: bfloat16 [16384, 1024], P(('group', 'loop'), 'mp'), may hold values from -0.046875 to 0.046875
- union_ids: int32 [128], replicated, may hold values from 0 to 8191, as said below
Outputs:
- grad_key: float32 [4, 2048, 1024], P('mp', ('group', 'loop'))
- grad_value: float32 [4, 2048, 1024], P('mp', ('group', 'loop'))
- union_key: float32 [128, 1024], replicated
- union_value: float32 [128, 1024], replicated
The draws below stay inside these ranges and needn't reach their ends.
Inputs may be any that keep to these rules, and one draw needn't show every extreme that they name: `union_ids`: 128 distinct row indices in increasing order, the first 0 and the last 8191.
All inputs are finite; a program needn't handle non-finite values.
Results may differ from the reference program's by a relative error of at most 0.0041.
Values may be sent and summed in bfloat16 or wider, within the bound.
No kernel may reach another device: no remote copies, remote signals or barrier semaphores. Data moves between devices by JAX's collectives and lax.ppermute only.
A program may use at most 128 MiB of HBM per device.

```python
import jax
import jax.numpy as jnp
from jax import lax

D = 8192
TOK = 128
OUT = 128
DATA = 128
TOKENS = 16384
KV = 1024
N_MP = 4


def draw_union_ids(key, part):
    key = jax.random.fold_in(key, 11)
    shuffled = jax.random.permutation(key, D - 2)
    middle = shuffled[:OUT - 2].astype(jnp.int32) + 1
    ends = jnp.array([0, D - 1], jnp.int32)
    return jnp.sort(jnp.concatenate([ends, middle])).astype(jnp.int32)


def draw_hidden_in(key, part):
    key = jax.random.fold_in(key, 5)
    column = jnp.arange(D, dtype=jnp.float32) / (D - 1.0)
    base = jax.random.truncated_normal(key, -6.0, 6.0, (TOKENS, D), jnp.float32)
    factor = jnp.power(3.0, column - 0.5)
    return (base * factor[None, :]).astype(jnp.bfloat16)


def block_scale(own_key, shape, split, smallest, largest):
    gain, own = 1.0, jax.random.fold_in(own_key, 6)
    for dim, parts in split:
        draws = jnp.exp(jax.random.uniform(jax.random.fold_in(own, dim), (parts,), jnp.float32, smallest / len(split), largest / len(split)))
        gain = gain * jnp.repeat(draws, shape[dim] // parts).reshape([-1 if axis == dim else 1 for axis in range(len(shape))])
    return gain


def bell_draw(stream_key, dims, deviation, most, split=(), kind=jnp.bfloat16):
    level = block_scale(stream_key, dims, split, -0.22, 0.18) if split else 1.0
    entries = jax.random.normal(stream_key, dims, jnp.float32) * deviation * level
    return jnp.minimum(jnp.maximum(entries, -most), most).astype(kind)


def setup_inputs(seed: int = 0) -> dict:
    keys = jax.random.split(jax.random.key(seed), 6)
    return {
        "hidden_in": draw_hidden_in(jax.random.fold_in(keys[5], 71), 0),
        "norm_gain": jnp.clip(1.0 + 0.1 * jax.random.normal(keys[1], (D,), jnp.float32), 0.5, 1.5),
        "key_cotangent": bell_draw(keys[2], (TOKENS, KV), (1.0 / TOKENS ** 0.5), 0.046875, ((0, 128), (1, 4))),
        "value_cotangent": bell_draw(keys[3], (TOKENS, KV), (1.0 / TOKENS ** 0.5), 0.046875, ((0, 128), (1, 4))),
        "union_ids": draw_union_ids(jax.random.fold_in(keys[5], 71), 0),
    }


def reference(hidden_in, norm_gain, key_cotangent, value_cotangent, union_ids):
    keep_rows = jnp.ones((D,), jnp.float32).at[union_ids].set(0.0)
    hidden_blocks = hidden_in.reshape(DATA, TOK, D)
    key_blocks = key_cotangent.reshape(DATA, TOK, KV)
    value_blocks = value_cotangent.reshape(DATA, TOK, KV)

    def one_block(carry, pieces):
        bulk_key, bulk_value, rows_key, rows_value = carry
        hidden_block, key_block, value_block = pieces
        hidden_f = hidden_block.astype(jnp.float32)
        mean_square = lax.optimization_barrier(jnp.mean(hidden_f * hidden_f, axis=-1, keepdims=True))
        normed = (hidden_f * lax.rsqrt(mean_square + 1e-05) * norm_gain).astype(jnp.bfloat16)
        partial_key = jnp.dot(normed.T, key_block, preferred_element_type=jnp.float32)
        partial_value = jnp.dot(normed.T, value_block, preferred_element_type=jnp.float32)
        term_key = lax.optimization_barrier((partial_key * keep_rows[:, None]).astype(jnp.bfloat16))
        term_value = lax.optimization_barrier((partial_value * keep_rows[:, None]).astype(jnp.bfloat16))
        bulk_key = bulk_key + term_key.astype(jnp.float32)
        bulk_value = bulk_value + term_value.astype(jnp.float32)
        rows_key = rows_key + partial_key[union_ids]
        rows_value = rows_value + partial_value[union_ids]
        return ((bulk_key, bulk_value, rows_key, rows_value), None)
    start = (jnp.zeros((D, KV), jnp.float32), jnp.zeros((D, KV), jnp.float32), jnp.zeros((OUT, KV), jnp.float32), jnp.zeros((OUT, KV), jnp.float32))
    final, unused = lax.scan(one_block, start, (hidden_blocks, key_blocks, value_blocks))
    grad_key = final[0].reshape(N_MP, D // N_MP, KV)
    grad_value = final[1].reshape(N_MP, D // N_MP, KV)
    return (grad_key, grad_value, final[2], final[3])
```

```python
import jax
import jax.numpy as jnp
from jax import lax
from jax.experimental import pallas as pl
from jax.experimental.pallas import tpu as pltpu
from jax.sharding import Mesh, PartitionSpec as P

AXES = ("y", "core", "x", "zh", "zl")
LANES = 128
VMEM = pl.BlockSpec(memory_space=pltpu.VMEM)
PARAMS = pltpu.CompilerParams(vmem_limit_bytes=40 * 1024 * 1024)


def split3(v):
    hi = v.astype(jnp.bfloat16).astype(jnp.float32)
    mid = (v - hi).astype(jnp.bfloat16).astype(jnp.float32)
    low = (v - hi - mid).astype(jnp.bfloat16).astype(jnp.float32)
    return hi, mid, low


def prepare(hidden_ref, key_ref, value_ref, ids_ref, gain_ref, out_ref):
    n_x, n_zl, _, _ = out_ref.shape
    toks, width = hidden_ref.shape
    n_union = ids_ref.shape[0]
    hidden = hidden_ref[...]
    hidden_f = hidden.astype(jnp.float32)
    squares = jnp.sum(hidden_f * hidden_f, axis=1, keepdims=True)
    hit = lax.broadcasted_iota(jnp.int32, (n_union, width), 1) == ids_ref[...]
    gains = jnp.sum(jnp.where(hit, gain_ref[...], 0.0), axis=1, keepdims=True)
    picked = lax.dot_general(
        jnp.where(hit, 1.0, 0.0).astype(jnp.bfloat16),
        hidden,
        (((1,), (1,)), ((), ())),
        preferred_element_type=jnp.float32,
    ).astype(jnp.bfloat16)
    lane = lax.broadcasted_iota(jnp.int32, (toks, LANES), 1)
    table = jnp.zeros((toks, LANES), jnp.float32)
    for place, part in enumerate(split3(squares) + split3(gains)):
        table = jnp.where(lane == place, part, table)
    extra = table.T[:16].astype(jnp.bfloat16)
    per = n_union // n_zl
    for x in range(n_x):
        source = key_ref if x < n_x // 2 else value_ref
        at = LANES * (x % (n_x // 2))
        block = source[:, at : at + LANES]
        for z in range(n_zl):
            out_ref[x, z, :toks] = block
            out_ref[x, z, toks : toks + per] = picked[per * z : per * (z + 1)]
            out_ref[x, z, toks + per :] = extra


def scale(features, in_ref, zl_ref, out_ref, union_ref, gain_ref):
    n_x, n_zl, rows, _ = in_ref.shape
    toks = LANES
    per = rows - toks - 16
    copies = out_ref.shape[0]
    zl = zl_ref[0]
    total = jnp.zeros((per, n_zl * LANES), jnp.float32)
    for x in range(n_x):
        extra = in_ref[x, 0, toks + per :].astype(jnp.float32)
        picked = in_ref[x, 0, toks : toks + per].astype(jnp.float32)
        for z in range(1, n_zl):
            extra = extra + in_ref[x, z, toks + per :].astype(jnp.float32)
            picked = picked + in_ref[x, z, toks : toks + per].astype(jnp.float32)
        if x == 0:
            gain = extra[3:4] + extra[4:5] + extra[5:6]
            gain_ref[...] = jnp.broadcast_to(gain, (LANES, LANES)).T
        squares = extra[0:1] + extra[1:2] + extra[2:3]
        inverse = lax.rsqrt(squares / features + 1e-05)
        column = jnp.broadcast_to(inverse, (LANES, LANES)).T
        gain_rows = gain_ref[pl.ds(pl.multiple_of(zl * per, 8), per), :]
        normed = (picked * inverse * gain_rows).astype(jnp.bfloat16)
        raw = jnp.concatenate([in_ref[x, z, :toks] for z in range(n_zl)], axis=1)
        total = total + jnp.dot(normed, raw, preferred_element_type=jnp.float32)
        for z in range(n_zl):
            scaled = (in_ref[x, z, :toks].astype(jnp.float32) * column).astype(jnp.bfloat16)
            for y in range(copies):
                out_ref[y, x, :, z * LANES : (z + 1) * LANES] = scaled
    for z in range(n_zl):
        union_ref[:, z, :] = total[:, z * LANES : (z + 1) * LANES]


def multiply(a_ref, b_ref, out_ref):
    rows = a_ref.shape[3]
    depth = a_ref.shape[1] * a_ref.shape[2]
    part = lax.dot_general(
        a_ref[0].reshape(depth, rows),
        b_ref[:, 0].reshape(depth, b_ref.shape[3]),
        (((0,), (0,)), ((), ())),
        preferred_element_type=jnp.float32,
    ).reshape(out_ref.shape)

    @pl.when(pl.program_id(0) == 0)
    def _():
        out_ref[...] = part

    @pl.when(pl.program_id(0) > 0)
    def _():
        out_ref[...] += part


def exchange(v, axes):
    return lax.all_to_all(v, axes, split_axis=0, concat_axis=0, tiled=True)


def gather(v, axes):
    count = lax.axis_size(axes)
    return exchange(jnp.broadcast_to(v[None], (count,) + v.shape), axes)


def per_device(hidden_in, norm_gain, key_cotangent, value_cotangent, union_ids):
    toks, width = hidden_in.shape
    n_y, n_core, n_x, n_zh, n_zl = (lax.axis_size(a) for a in AXES)
    y, core, x, zh, zl = (lax.axis_index(a) for a in AXES)
    n_union = union_ids.shape[0]
    heads = 2 * key_cotangent.shape[1]
    tile = width // n_y
    cols = n_zl * LANES
    per = n_union // n_zl

    a_sent = jnp.swapaxes(hidden_in.reshape(toks, n_y, tile), 0, 1)
    a_rows = exchange(a_sent, "y")

    local_ids = (union_ids - zl * width).reshape(n_union, 1)
    packed = pl.pallas_call(
        prepare,
        out_shape=jax.ShapeDtypeStruct((n_x, n_zl, toks + per + 16, LANES), jnp.bfloat16),
        in_specs=[VMEM] * 5,
        out_specs=VMEM,
        compiler_params=PARAMS,
    )(hidden_in, key_cotangent, value_cotangent, local_ids, norm_gain.reshape(1, width))
    packed = exchange(packed.reshape((n_x * n_zl,) + packed.shape[2:]), ("x", "zl"))
    packed = packed.reshape((n_x, n_zl) + packed.shape[1:])

    b_sent, union_part = pl.pallas_call(
        lambda *refs: scale(float(width * n_zl), *refs),
        out_shape=(
            jax.ShapeDtypeStruct((n_y, n_x, toks, cols), jnp.bfloat16),
            jax.ShapeDtypeStruct((per, n_zl, LANES), jnp.float32),
        ),
        in_specs=[VMEM, pl.BlockSpec(memory_space=pltpu.SMEM)],
        out_specs=(VMEM, VMEM),
        scratch_shapes=[pltpu.VMEM((LANES, LANES), jnp.float32)],
        compiler_params=PARAMS,
    )(packed, zl.astype(jnp.int32).reshape(1))

    a_all = gather(a_rows, "x")
    b_all = exchange(b_sent, "y")

    union_sum = jnp.sum(exchange(union_part, ("y", "core", "zh")), axis=0).astype(jnp.bfloat16)
    union_line = gather(union_sum, ("zh", "zl"))
    union_all = gather(union_line, ("y", "core", "x"))
    union_all = union_all.reshape(n_y * n_core, 2, n_x // 2, n_zh, n_zl, n_zl, LANES)
    union_all = jnp.transpose(union_all, (1, 4, 0, 3, 5, 2, 6)).astype(jnp.float32)
    union_all = union_all.reshape(2, n_union, heads * n_zl // 2)

    product = pl.pallas_call(
        multiply,
        grid=(n_x,),
        out_shape=jax.ShapeDtypeStruct((n_core, tile // n_core, cols), jnp.float32),
        in_specs=[
            pl.BlockSpec((1, n_y, toks, tile), lambda i: (i, 0, 0, 0)),
            pl.BlockSpec((n_y, 1, toks, cols), lambda i: (0, i, 0, 0)),
        ],
        out_specs=pl.BlockSpec((n_core, tile // n_core, cols), lambda i: (0, 0, 0)),
        compiler_params=PARAMS,
    )(a_all, b_all)
    product = jnp.sum(exchange(product, "core"), axis=0).astype(jnp.bfloat16)
    own = tile // (n_core * n_x * n_zh)
    pieces = exchange(product.reshape(n_x * n_zh, own, cols), ("x", "zh"))
    summed = jnp.sum(pieces.reshape(n_x, n_zh, own, cols).astype(jnp.float32), axis=1)
    first = own * (((y * n_core + core) * n_x + x) * n_zh + zh)
    gain = lax.dynamic_slice(norm_gain, (first,), (own,))
    row_ids = zl * width + first + lax.iota(jnp.int32, own)
    outlier = jnp.any(row_ids[:, None] == union_ids[None, :], axis=1)
    summed = jnp.where(outlier[None, :, None], 0.0, summed * gain[None, :, None])
    summed = summed.reshape(2, n_x // 2, own, n_zl, LANES)
    grads = jnp.transpose(summed, (0, 2, 3, 1, 4)).reshape(2, 1, own, heads * n_zl // 2)
    return (grads[0], grads[1], union_all[0], union_all[1])


def solution(mesh):
    sizes = dict(mesh.shape)
    split = Mesh(
        mesh.devices.reshape(sizes["group"] // 2, 2, 4, sizes["loop"] // 4, sizes["mp"]), AXES
    )
    rows = ("y", "core", "x", "zh")
    return jax.shard_map(
        per_device,
        mesh=split,
        in_specs=(P(rows, "zl"), P("zl"), P(rows, "zl"), P(rows, "zl"), P()),
        out_specs=(P("zl", rows, None), P("zl", rows, None), P(), P()),
        check_vma=False,
    )
```

```python
import jax
import jax.numpy as jnp
from jax import lax
from jax.experimental import pallas as pl
from jax.experimental.pallas import tpu as pltpu
from jax.sharding import Mesh, PartitionSpec as P

AXES = ("y", "core", "x", "zh", "zl")
LANES = 128
AUX = 16
VMEM = pl.BlockSpec(memory_space=pltpu.VMEM)
SMEM = pl.BlockSpec(memory_space=pltpu.SMEM)
PARAMS = pltpu.CompilerParams(vmem_limit_bytes=40 * 1024 * 1024)


def split3(v):
    hi = v.astype(jnp.bfloat16).astype(jnp.float32)
    mid = (v - hi).astype(jnp.bfloat16).astype(jnp.float32)
    low = (v - hi - mid).astype(jnp.bfloat16).astype(jnp.float32)
    return hi, mid, low


def column(row):
    return jnp.broadcast_to(row, (LANES, LANES)).T


def spread_cotangents(key_ref, value_ref, out_ref):
    n_x, n_zl, _, _ = out_ref.shape
    for x in range(n_x):
        source = key_ref if x < n_x // 2 else value_ref
        at = LANES * (x % (n_x // 2))
        for z in range(n_zl):
            out_ref[x, z] = source[:, at : at + LANES]


def prepare(y_ref, zl_ref, hidden_ref, ids_ref, gain_ref, *refs):
    outs, picked_ref = refs[:-1], refs[-1]
    n_y = len(outs)
    toks, width = hidden_ref.shape
    tile = width // n_y
    n_union = ids_ref.shape[1]
    per = n_union // n_y
    hidden = hidden_ref[...]
    hidden_f = hidden.astype(jnp.float32)
    squares = jnp.sum(hidden_f * hidden_f, axis=1, keepdims=True)
    ids = column(ids_ref[...].astype(jnp.float32))[:, :1].astype(jnp.int32) - zl_ref[0] * width
    hit = lax.broadcasted_iota(jnp.int32, (n_union, width), 1) == ids
    gains = jnp.sum(jnp.where(hit, gain_ref[...], 0.0), axis=1, keepdims=True)
    picked_ref[...] = lax.dot_general(
        jnp.where(hit, 1.0, 0.0).astype(jnp.bfloat16),
        hidden,
        (((1,), (1,)), ((), ())),
        preferred_element_type=jnp.float32,
    ).astype(jnp.bfloat16)
    lane = lax.broadcasted_iota(jnp.int32, (toks, LANES), 1)
    table = jnp.zeros((toks, LANES), jnp.float32)
    for place, part in enumerate(split3(squares) + split3(gains)):
        table = jnp.where(lane == place, part, table)
    extra = table.T[:AUX].astype(jnp.bfloat16)
    for k, out_ref in enumerate(outs):
        to = lax.rem(y_ref[0] + k, n_y)
        out_ref[:toks] = hidden_ref[:, pl.ds(pl.multiple_of(to * tile, tile), tile)]
        for half in range(2):
            rows = pl.ds(pl.multiple_of(to * per + half * AUX, AUX), AUX)
            out_ref[toks:, half * LANES : (half + 1) * LANES] = picked_ref[rows, :]
        out_ref[toks:, 2 * LANES : 3 * LANES] = extra
        out_ref[toks:, 3 * LANES :] = jnp.zeros((AUX, tile - 3 * LANES), jnp.bfloat16)


def complete(features, n_y, *refs):
    blocks, parts, out_ref = refs[:n_y], refs[n_y:-1], refs[-1]
    toks = blocks[0].shape[0] - AUX
    for k in range(n_y):
        out_ref[k, :toks] = blocks[k][:toks]
        rows = parts[0][k].astype(jnp.float32)
        for part in parts[1:]:
            rows = rows + part[k].astype(jnp.float32)
        extra = rows[:, 2 * LANES : 3 * LANES]
        squares = extra[0:1] + extra[1:2] + extra[2:3]
        scales = split3(lax.rsqrt(squares / features + 1e-05))
        place = lax.broadcasted_iota(jnp.int32, (AUX, LANES), 0)
        for i, part in enumerate(scales):
            extra = jnp.where(place == i, part, extra)
        out_ref[k, toks:, : 2 * LANES] = rows[:, : 2 * LANES].astype(jnp.bfloat16)
        out_ref[k, toks:, 2 * LANES : 3 * LANES] = extra.astype(jnp.bfloat16)
        out_ref[k, toks:, 3 * LANES :] = rows[:, 3 * LANES :].astype(jnp.bfloat16)


def multiply(y_ref, x_ref, core_ref, gain_ref, b_ref, *refs):
    own_ref, other_ref, bulk_ref, union_ref, gains_ref = refs[-5:]
    blocks = refs[:-5]
    n_y, n_x, toks, cols = b_ref.shape
    tile = bulk_ref.shape[0]
    per = union_ref.shape[0]
    y, x = y_ref[0], x_ref[0]
    gain = gain_ref[:, pl.ds(pl.multiple_of(y * tile, tile), tile)]
    extra = blocks[0][0, toks:, 2 * LANES : 3 * LANES].astype(jnp.float32)
    gains_ref[...] = column(extra[3:4] + extra[4:5] + extra[5:6])
    union_gain = gains_ref[pl.ds(pl.multiple_of(y * per, per), per), :]
    for j, block in enumerate(blocks):
        from_x = lax.rem(x + n_x - j, n_x)
        normed, picked, right = [], [], []
        for k in range(n_y):
            from_y = lax.rem(y + n_y - k, n_y)
            right.append(b_ref[from_y, from_x])
            extra = block[k, toks:, 2 * LANES : 3 * LANES].astype(jnp.float32)
            scale = extra[0:1] + extra[1:2] + extra[2:3]
            scales = column(scale)
            scales = jnp.concatenate([scales] * (tile // LANES), axis=1)
            normed.append((block[k, :toks].astype(jnp.float32) * scales * gain).astype(jnp.bfloat16))
            raw = block[k, toks:].astype(jnp.float32)
            raw = jnp.concatenate([raw[:, :LANES], raw[:, LANES : 2 * LANES]], axis=0)
            picked.append((raw * scale * union_gain).astype(jnp.bfloat16))
        right = jnp.concatenate(right, axis=0)
        bulk = lax.dot_general(
            jnp.concatenate(normed, axis=0),
            right,
            (((0,), (0,)), ((), ())),
            preferred_element_type=jnp.float32,
        )
        union = jnp.dot(jnp.concatenate(picked, axis=1), right, preferred_element_type=jnp.float32)
        if j == 0:
            bulk_ref[...] = bulk
            union_ref[...] = union
        else:
            bulk_ref[...] += bulk
            union_ref[...] += union
    rows, outliers = tile // 2, per // 2
    for out_ref, core in ((own_ref, core_ref[0]), (other_ref, 1 - core_ref[0])):
        out_ref[:rows] = bulk_ref[pl.ds(pl.multiple_of(core * rows, rows), rows), :]
        out_ref[rows:] = union_ref[pl.ds(pl.multiple_of(core * outliers, outliers), outliers), :]


def add_cores(own_ref, got_ref, out_ref):
    n_x, n_zh, rows, _ = out_ref.shape
    bulk = n_x * n_zh * rows
    cols = own_ref.shape[1]
    outliers = (own_ref[bulk:] + got_ref[bulk:]).astype(jnp.bfloat16)
    wide = cols // n_x
    for x in range(n_x):
        for z in range(n_zh):
            at = rows * (x * n_zh + z)
            out_ref[x, z, :, :cols] = (own_ref[at : at + rows] + got_ref[at : at + rows]).astype(jnp.bfloat16)
            out_ref[x, z, :, cols:] = outliers[:, x * wide : (x + 1) * wide]


def finish(first_ref, ids_ref, in_ref, key_ref, value_ref, union_ref):
    n_x, n_zh, rows, _ = in_ref.shape
    n_zl = key_ref.shape[2] // (2 * LANES)
    cols = n_zl * LANES
    row = lax.broadcasted_iota(jnp.int32, (rows, LANES), 0) + first_ref[0]
    hits = jnp.sum(jnp.where(row == ids_ref[...], 1.0, 0.0), axis=1, keepdims=True)
    for x in range(n_x):
        total = in_ref[x, 0].astype(jnp.float32)
        for z in range(1, n_zh):
            total = total + in_ref[x, z].astype(jnp.float32)
        kind, half = x // 2, x % 2
        out_ref = value_ref if kind else key_ref
        for z in range(n_zl):
            at = LANES * (2 * z + half)
            out_ref[0, :, at : at + LANES] = jnp.where(hits > 0.0, 0.0, total[:, z * LANES : (z + 1) * LANES])
        outliers = total[:, cols:].astype(jnp.bfloat16)
        for i in range(union_ref.shape[0]):
            union_ref[i, kind, :, half * LANES : (half + 1) * LANES] = outliers


def lay_out(in_ref, key_ref, value_ref):
    count, _, rows, cols = in_ref.shape
    n_x = key_ref.shape[1] // cols
    for i in range(count):
        at, to = rows * (i // n_x), cols * (i % n_x)
        key_ref[at : at + rows, to : to + cols] = in_ref[i, 0].astype(jnp.float32)
        value_ref[at : at + rows, to : to + cols] = in_ref[i, 1].astype(jnp.float32)


def call(body, out_shape, args, scalars=0, scratch=()):
    single = not isinstance(out_shape, tuple)
    return pl.pallas_call(
        body,
        out_shape=out_shape,
        in_specs=[SMEM] * scalars + [VMEM] * (len(args) - scalars),
        out_specs=VMEM if single else tuple(VMEM for _ in out_shape),
        scratch_shapes=scratch,
        compiler_params=PARAMS,
    )(*args)


def exchange(v, axes):
    return lax.all_to_all(v, axes, split_axis=0, concat_axis=0, tiled=True)


def shift(v, axis, by):
    count = lax.axis_size(axis)
    return lax.ppermute(v, axis, [(i, (i + by) % count) for i in range(count)])


def per_device(hidden_in, norm_gain, key_cotangent, value_cotangent, union_ids):
    bf16, f32 = jnp.bfloat16, jnp.float32
    toks, width = hidden_in.shape
    n_y, n_core, n_x, n_zh, n_zl = (lax.axis_size(a) for a in AXES)
    y, core, x, zh, zl = (lax.axis_index(a).astype(jnp.int32) for a in AXES)
    n_union = union_ids.shape[0]
    heads = key_cotangent.shape[1] * n_zl
    tile = width // n_y
    cols = n_zl * LANES
    per = n_union // n_y
    shape = jax.ShapeDtypeStruct
    ids = union_ids.reshape(1, n_union)
    gain = norm_gain.reshape(1, width)
    at_y, at_x, at_core, at_zl = (v.reshape(1) for v in (y, x, core, zl))

    spread = call(spread_cotangents, shape((n_x, n_zl, toks, LANES), bf16), (key_cotangent, value_cotangent))
    b_some = exchange(spread.reshape(n_x * n_zl, toks, LANES), ("x", "zl"))
    b_some = jnp.swapaxes(b_some.reshape(n_x, n_zl, toks, LANES), 1, 2).reshape(n_x, toks, cols)
    b_all = exchange(jnp.broadcast_to(b_some[None], (n_y,) + b_some.shape), "y")

    sent = call(
        prepare,
        tuple(shape((toks + AUX, tile), bf16) for _ in range(n_y)),
        (at_y, at_zl, hidden_in, ids, gain),
        2,
        [pltpu.VMEM((n_union, toks), bf16)],
    )
    blocks = [sent[0]] + [shift(sent[k], "y", k) for k in range(1, n_y)]
    aux = jnp.stack([block[toks:] for block in blocks])
    parts = [aux] + [shift(aux, "zl", k) for k in range(1, n_zl)]
    a_own = call(
        lambda *refs: complete(float(width * n_zl), n_y, *refs),
        shape((n_y, toks + AUX, tile), bf16),
        (*blocks, *parts),
    )
    a_all = [a_own] + [shift(a_own, "x", k) for k in range(1, n_x)]

    half = shape(((tile + per) // n_core, cols), f32)
    own, other = call(
        multiply,
        (half, half),
        (at_y, at_x, at_core, gain, b_all, *a_all),
        3,
        [pltpu.VMEM((tile, cols), f32), pltpu.VMEM((per, cols), f32), pltpu.VMEM((LANES, LANES), f32)],
    )
    got = shift(other, "core", 1)
    rows = tile // (n_core * n_x * n_zh)
    pieces = call(add_cores, shape((n_x, n_zh, rows, cols + cols // n_x), bf16), (own, got))
    pieces = exchange(pieces.reshape((n_x * n_zh,) + pieces.shape[2:]), ("x", "zh"))
    first = zl * width + rows * (((y * n_core + core) * n_x + x) * n_zh + zh)
    grad = shape((1, rows, heads), f32)
    grad_key, grad_value, outliers = call(
        finish,
        (grad, grad, shape((n_y * n_core * n_x, 2, per // n_core, 2 * LANES), bf16)),
        (first.reshape(1), ids, pieces.reshape((n_x, n_zh) + pieces.shape[1:])),
        1,
    )
    outliers = exchange(outliers, ("y", "core", "x"))
    union = shape((n_union, heads), f32)
    union_key, union_value = call(lay_out, (union, union), (outliers,))
    return (grad_key, grad_value, union_key, union_value)


def solution(mesh):
    sizes = dict(mesh.shape)
    split = Mesh(
        mesh.devices.reshape(sizes["group"] // 2, 2, 4, sizes["loop"] // 4, sizes["mp"]), AXES
    )
    rows = ("y", "core", "x", "zh")
    return jax.shard_map(
        per_device,
        mesh=split,
        in_specs=(P(rows, "zl"), P("zl"), P(rows, "zl"), P(rows, "zl"), P()),
        out_specs=(P("zl", rows, None), P("zl", rows, None), P(), P()),
        check_vma=False,
    )
```

```python
import jax
import jax.numpy as jnp
from jax import lax
from jax.experimental import pallas as pl
from jax.experimental.pallas import tpu as pltpu
from jax.sharding import Mesh, PartitionSpec as P

AXES = ("y", "core", "x", "zh", "zl")
LANES = 128
AUX = 16
VMEM = pl.BlockSpec(memory_space=pltpu.VMEM)
SMEM = pl.BlockSpec(memory_space=pltpu.SMEM)
PARAMS = pltpu.CompilerParams(vmem_limit_bytes=20 * 1024 * 1024)


def split3(v):
    hi = v.astype(jnp.bfloat16).astype(jnp.float32)
    mid = (v - hi).astype(jnp.bfloat16).astype(jnp.float32)
    low = (v - hi - mid).astype(jnp.bfloat16).astype(jnp.float32)
    return hi, mid, low


def column(row):
    return jnp.broadcast_to(row, (LANES, LANES)).T


def prepare(zl_ref, hidden_in, key_in, value_in, ids_in, gain_in, *refs):
    packed_ref, hidden_ref, key_ref, value_ref, ids_ref, gain_ref, sems = refs
    copies = [
        pltpu.make_async_copy(source, target, sems.at[i])
        for i, (source, target) in enumerate(
            [
                (hidden_in, hidden_ref),
                (key_in, key_ref),
                (value_in, value_ref),
                (ids_in, ids_ref),
                (gain_in, gain_ref),
            ]
        )
    ]
    for copy in copies:
        copy.start()
    n_x, n_zl, _, _ = packed_ref.shape
    toks, width = hidden_ref.shape
    n_union = ids_ref.shape[1]
    per = n_union // n_zl
    for copy in copies[1:]:
        copy.wait()
    for x in range(n_x):
        source = key_ref if x < n_x // 2 else value_ref
        at = LANES * (x % (n_x // 2))
        for z in range(n_zl):
            packed_ref[x, z, :toks] = source[:, at : at + LANES]
    ids = column(ids_ref[...].astype(jnp.float32))[:, :1].astype(jnp.int32) - zl_ref[0] * width
    hit = lax.broadcasted_iota(jnp.int32, (n_union, width), 1) == ids
    gains = jnp.sum(jnp.where(hit, gain_ref[...], 0.0), axis=1, keepdims=True)
    copies[0].wait()
    hidden = hidden_ref[...]
    hidden_f = hidden.astype(jnp.float32)
    squares = jnp.sum(hidden_f * hidden_f, axis=1, keepdims=True)
    picked = lax.dot_general(
        jnp.where(hit, 1.0, 0.0).astype(jnp.bfloat16),
        hidden,
        (((1,), (1,)), ((), ())),
        preferred_element_type=jnp.float32,
    ).astype(jnp.bfloat16)
    lane = lax.broadcasted_iota(jnp.int32, (toks, LANES), 1)
    table = jnp.zeros((toks, LANES), jnp.float32)
    for place, part in enumerate(split3(squares) + split3(gains)):
        table = jnp.where(lane == place, part, table)
    extra = table.T[:AUX].astype(jnp.bfloat16)
    for x in range(n_x):
        for z in range(n_zl):
            packed_ref[x, z, toks : toks + per] = picked[per * z : per * (z + 1)]
            packed_ref[x, z, toks + per :] = extra


def unpack(features, zl_ref, in_ref, out_ref, scale_ref, union_ref, gain_ref):
    n_x, n_zl, rows, _ = in_ref.shape
    toks = LANES
    per = rows - toks - AUX
    total = jnp.zeros((per, n_zl * LANES), jnp.float32)
    for x in range(n_x):
        extra = in_ref[x, 0, toks + per :].astype(jnp.float32)
        picked = in_ref[x, 0, toks : toks + per].astype(jnp.float32)
        for z in range(1, n_zl):
            extra = extra + in_ref[x, z, toks + per :].astype(jnp.float32)
            picked = picked + in_ref[x, z, toks : toks + per].astype(jnp.float32)
        if x == 0:
            gain_ref[...] = column(extra[3:4] + extra[4:5] + extra[5:6])
        squares = extra[0:1] + extra[1:2] + extra[2:3]
        scale = lax.rsqrt(squares / features + 1e-05)
        gains = gain_ref[pl.ds(pl.multiple_of(zl_ref[0] * per, per), per), :]
        normed = (picked * scale * gains).astype(jnp.bfloat16)
        right = jnp.concatenate([in_ref[x, z, :toks] for z in range(n_zl)], axis=1)
        total = total + jnp.dot(normed, right, preferred_element_type=jnp.float32)
        out_ref[x] = right
        table = jnp.zeros((AUX // 2, LANES), jnp.float32) + scale
        scale_ref[:, x * LANES : (x + 1) * LANES] = table
    count, few, _ = union_ref.shape
    for i in range(count):
        union_ref[i] = total[i * few : (i + 1) * few]


def sum_spread(groups, in_ref, out_ref):
    count = in_ref.shape[0]
    rest = count // groups
    few = in_ref.shape[1]
    for j in range(rest):
        total = in_ref[j].astype(jnp.float32)
        for i in range(1, groups):
            total = total + in_ref[i * rest + j].astype(jnp.float32)
        total = total.astype(jnp.bfloat16)
        for to in range(out_ref.shape[0]):
            out_ref[to, j * few : (j + 1) * few] = total


def multiply(x_ref, core_ref, gain_ref, scale_ref, right_ref, *refs):
    own_ref, other_ref, total_ref = refs[-3:]
    lefts = refs[:-3]
    n_x, n_y = len(lefts), own_ref.shape[0]
    toks, width = lefts[0].shape
    tile = width // n_y
    columns = []
    for j in range(n_x):
        x = lax.rem(x_ref[0] + n_x - j, n_x)
        columns.append(column(scale_ref[:1, pl.ds(pl.multiple_of(x * LANES, LANES), LANES)]))
    for y in range(n_y):
        at = slice(y * tile, (y + 1) * tile)
        normed, right = [], []
        for j, left_ref in enumerate(lefts):
            x = lax.rem(x_ref[0] + n_x - j, n_x)
            scales = jnp.concatenate([columns[j]] * (tile // LANES), axis=1)
            left = left_ref[:, at].astype(jnp.float32) * scales * gain_ref[:, at]
            normed.append(left.astype(jnp.bfloat16))
            right.append(right_ref[x])
        total_ref[...] = lax.dot_general(
            jnp.concatenate(normed, axis=0),
            jnp.concatenate(right, axis=0),
            (((0,), (0,)), ((), ())),
            preferred_element_type=jnp.float32,
        )
        rows = tile // 2
        for out_ref, core in ((own_ref, core_ref[0]), (other_ref, 1 - core_ref[0])):
            out_ref[y] = total_ref[pl.ds(pl.multiple_of(core * rows, rows), rows), :]


def add_cores(own_ref, got_ref, union_ref, out_ref):
    n_y, n_x, rows, _ = out_ref.shape
    rows -= union_ref.shape[1]
    for y in range(n_y):
        for x in range(n_x):
            at = slice(x * rows, (x + 1) * rows)
            out_ref[y, x, :rows] = (own_ref[y, at] + got_ref[y, at]).astype(jnp.bfloat16)
            out_ref[y, x, rows:] = union_ref[0]


def add_y(in_ref, out_ref, union_ref):
    n_y, n_x, _, _ = in_ref.shape
    n_zh, _, rows, _ = out_ref.shape
    for x in range(n_x):
        for z in range(n_zh):
            at = slice(z * rows, (z + 1) * rows)
            total = in_ref[0, x, at].astype(jnp.float32)
            for y in range(1, n_y):
                total = total + in_ref[y, x, at].astype(jnp.float32)
            out_ref[z, x] = total.astype(jnp.bfloat16)
        for y in range(n_y):
            union_ref[y, x] = in_ref[y, x, n_zh * rows :]


def finish(first_ref, ids_ref, in_ref, key_ref, value_ref):
    n_zh, n_x, rows, cols = in_ref.shape
    row = lax.broadcasted_iota(jnp.int32, (rows, LANES), 0) + first_ref[0]
    hits = jnp.sum(jnp.where(row == ids_ref[...], 1.0, 0.0), axis=1, keepdims=True)
    for x in range(n_x):
        total = in_ref[0, x].astype(jnp.float32)
        for z in range(1, n_zh):
            total = total + in_ref[z, x].astype(jnp.float32)
        total = jnp.where(hits > 0.0, 0.0, total)
        out_ref = value_ref if x // 2 else key_ref
        for z in range(cols // LANES):
            at = LANES * (2 * z + x % 2)
            out_ref[0, :, at : at + LANES] = total[:, z * LANES : (z + 1) * LANES]


def lay_out(n_zl, core_ref, own_ref, got_ref, key_ref, value_ref):
    n_y, n_x, rows, cols = own_ref.shape
    few = rows // n_zl
    per = key_ref.shape[0] // n_zl
    first = core_ref[0] == 0
    for x in range(n_x):
        out_ref = value_ref if x // 2 else key_ref
        blocks = []
        for y in range(n_y):
            own, got = own_ref[y, x].astype(jnp.float32), got_ref[y, x].astype(jnp.float32)
            blocks += [jnp.where(first, own, got), jnp.where(first, got, own)]
        for z in range(n_zl):
            lines = jnp.concatenate([block[few * z : few * (z + 1)] for block in blocks], axis=0)
            for j in range(cols // LANES):
                at = LANES * (2 * j + x % 2)
                out_ref[per * z : per * (z + 1), at : at + LANES] = lines[:, j * LANES : (j + 1) * LANES]


def call(body, out_shape, args, scalars=0, scratch=(), cost=0):
    single = not isinstance(out_shape, tuple)
    return pl.pallas_call(
        body,
        out_shape=out_shape,
        in_specs=[SMEM] * scalars + [VMEM] * (len(args) - scalars),
        out_specs=VMEM if single else tuple(VMEM for _ in out_shape),
        scratch_shapes=scratch,
        cost_estimate=pl.CostEstimate(flops=0, bytes_accessed=cost, transcendentals=0) if cost else None,
        compiler_params=PARAMS,
    )(*args)


def exchange(v, axes):
    return lax.all_to_all(v, axes, split_axis=0, concat_axis=0, tiled=True)


def shift(v, axis, by):
    count = lax.axis_size(axis)
    return lax.ppermute(v, axis, [(i, (i + by) % count) for i in range(count)])


def per_device(hidden_in, norm_gain, key_cotangent, value_cotangent, union_ids):
    bf16, f32 = jnp.bfloat16, jnp.float32
    toks, width = hidden_in.shape
    n_y, n_core, n_x, n_zh, n_zl = (lax.axis_size(a) for a in AXES)
    y, core, x, zh, zl = (lax.axis_index(a).astype(jnp.int32) for a in AXES)
    n_union = union_ids.shape[0]
    heads = key_cotangent.shape[1] * n_zl
    cols = n_zl * LANES
    per = n_union // n_zl
    shape = jax.ShapeDtypeStruct
    ids = union_ids.reshape(1, n_union)
    gain = norm_gain.reshape(1, width)
    at_y, at_x, at_core, at_zl = (v.reshape(1) for v in (y, x, core, zl))

    inputs = (hidden_in, key_cotangent, value_cotangent, ids, gain)
    packed = pl.pallas_call(
        prepare,
        out_shape=shape((n_x, n_zl, toks + per + AUX, LANES), bf16),
        in_specs=[SMEM] + [pl.BlockSpec(memory_space=pl.ANY)] * len(inputs),
        out_specs=VMEM,
        scratch_shapes=[pltpu.VMEM(v.shape, v.dtype) for v in inputs]
        + [pltpu.SemaphoreType.DMA((len(inputs),))],
        compiler_params=pltpu.CompilerParams(vmem_limit_bytes=60 * 1024 * 1024),
    )(at_zl, *inputs)
    packed = exchange(packed.reshape((n_x * n_zl,) + packed.shape[2:]), ("x", "zl"))
    few = per // (n_y * n_core)
    right, scale, outliers = call(
        lambda *refs: unpack(float(width * n_zl), *refs),
        (
            shape((n_x, toks, cols), bf16),
            shape((AUX // 2, n_x * LANES), f32),
            shape((n_y * n_core, few, cols), f32),
        ),
        (at_zl, packed.reshape((n_x, n_zl) + packed.shape[1:])),
        1,
        [pltpu.VMEM((LANES, LANES), f32)],
    )
    left = [hidden_in] + [shift(hidden_in, "x", k) for k in range(1, n_x)]

    outliers = exchange(outliers, ("y", "core"))
    outliers = call(
        lambda *refs: sum_spread(n_y * n_core, *refs),
        shape((n_zh * n_zl, few, cols), bf16),
        (outliers,),
    )
    outliers = exchange(outliers, ("zh", "zl"))
    outliers = call(
        lambda *refs: sum_spread(n_zh, *refs),
        shape((1, n_zl * few, cols), bf16),
        (outliers,),
    )

    half = shape((n_y, width // (n_y * n_core), cols), f32)
    own, other = call(
        multiply,
        (half, half),
        (at_x, at_core, gain, scale, right, *left),
        2,
        [pltpu.VMEM((width // n_y, cols), f32)],
        cost=128 * 1024 * 1024,
    )
    other, outliers = lax.optimization_barrier((other, outliers))
    got = shift(other, "core", 1)
    rows = width // (n_y * n_core * n_x * n_zh)
    lines = n_zh * rows + n_zl * few
    pieces = call(add_cores, shape((n_y, n_x, lines, cols), bf16), (own, got, outliers))
    pieces = exchange(pieces.reshape(n_y * n_x, lines, cols), ("y", "x"))
    pieces, outliers = call(
        add_y,
        (shape((n_zh, n_x, rows, cols), bf16), shape((n_y, n_x, n_zl * few, cols), bf16)),
        (pieces.reshape(n_y, n_x, lines, cols),),
    )
    union = shape((n_union, heads), f32)
    union_key, union_value = call(
        lambda *refs: lay_out(n_zl, *refs),
        (union, union),
        (at_core, outliers, shift(outliers, "core", 1)),
        1,
    )
    pieces = exchange(pieces, "zh")
    first = zl * width + rows * (((y * n_core + core) * n_x + x) * n_zh + zh)
    grad = shape((1, rows, heads), f32)
    grad_key, grad_value = call(finish, (grad, grad), (first.reshape(1), ids, pieces), 1)
    return (grad_key, grad_value, union_key, union_value)


def solution(mesh):
    sizes = dict(mesh.shape)
    split = Mesh(
        mesh.devices.reshape(sizes["group"] // 2, 2, 4, sizes["loop"] // 4, sizes["mp"]), AXES
    )
    rows = ("y", "core", "x", "zh")
    return jax.shard_map(
        per_device,
        mesh=split,
        in_specs=(P(rows, "zl"), P("zl"), P(rows, "zl"), P(rows, "zl"), P()),
        out_specs=(P("zl", rows, None), P("zl", rows, None), P(), P()),
        check_vma=False,
    )
```

```python
import jax
import jax.numpy as jnp
from jax import lax
from jax.experimental import pallas as pl
from jax.experimental.pallas import tpu as pltpu
from jax.sharding import Mesh, PartitionSpec as P

AXES = ("y", "core", "x", "zh", "zl")
LANES = 128
AUX = 16
VMEM = pl.BlockSpec(memory_space=pltpu.VMEM)
SMEM = pl.BlockSpec(memory_space=pltpu.SMEM)
PARAMS = pltpu.CompilerParams(vmem_limit_bytes=20 * 1024 * 1024)


def split3(v):
    hi = v.astype(jnp.bfloat16).astype(jnp.float32)
    mid = (v - hi).astype(jnp.bfloat16).astype(jnp.float32)
    low = (v - hi - mid).astype(jnp.bfloat16).astype(jnp.float32)
    return hi, mid, low


def column(row):
    return jnp.broadcast_to(row, (LANES, LANES)).T


def prepare(zl_ref, hidden_in, key_in, value_in, ids_in, gain_in, *refs):
    packed_ref, hidden_ref, key_ref, value_ref, ids_ref, gain_ref, sems = refs
    copies = [
        pltpu.make_async_copy(source, target, sems.at[i])
        for i, (source, target) in enumerate(
            [
                (hidden_in, hidden_ref),
                (key_in, key_ref),
                (value_in, value_ref),
                (ids_in, ids_ref),
                (gain_in, gain_ref),
            ]
        )
    ]
    for copy in copies:
        copy.start()
    n_x, n_zl, _, _ = packed_ref.shape
    toks, width = hidden_ref.shape
    n_union = ids_ref.shape[1]
    per = n_union // n_zl
    for copy in copies[1:]:
        copy.wait()
    for x in range(n_x):
        source = key_ref if x < n_x // 2 else value_ref
        at = LANES * (x % (n_x // 2))
        for z in range(n_zl):
            packed_ref[x, z, :toks] = source[:, at : at + LANES]
    ids = column(ids_ref[...].astype(jnp.float32))[:, :1].astype(jnp.int32) - zl_ref[0] * width
    hit = lax.broadcasted_iota(jnp.int32, (n_union, width), 1) == ids
    gains = jnp.sum(jnp.where(hit, gain_ref[...], 0.0), axis=1, keepdims=True)
    copies[0].wait()
    hidden = hidden_ref[...]
    hidden_f = hidden.astype(jnp.float32)
    squares = jnp.sum(hidden_f * hidden_f, axis=1, keepdims=True)
    picked = lax.dot_general(
        jnp.where(hit, 1.0, 0.0).astype(jnp.bfloat16),
        hidden,
        (((1,), (1,)), ((), ())),
        preferred_element_type=jnp.float32,
    ).astype(jnp.bfloat16)
    lane = lax.broadcasted_iota(jnp.int32, (toks, LANES), 1)
    table = jnp.zeros((toks, LANES), jnp.float32)
    for place, part in enumerate(split3(squares) + split3(gains)):
        table = jnp.where(lane == place, part, table)
    extra = table.T[:AUX].astype(jnp.bfloat16)
    for x in range(n_x):
        for z in range(n_zl):
            packed_ref[x, z, toks : toks + per] = picked[per * z : per * (z + 1)]
            packed_ref[x, z, toks + per :] = extra


def unpack(features, zl_ref, in_ref, out_ref, scale_ref, union_ref, gain_ref):
    n_x, n_zl, rows, _ = in_ref.shape
    toks = LANES
    per = rows - toks - AUX
    total = jnp.zeros((per, n_zl * LANES), jnp.float32)
    for x in range(n_x):
        extra = in_ref[x, 0, toks + per :].astype(jnp.float32)
        picked = in_ref[x, 0, toks : toks + per].astype(jnp.float32)
        for z in range(1, n_zl):
            extra = extra + in_ref[x, z, toks + per :].astype(jnp.float32)
            picked = picked + in_ref[x, z, toks : toks + per].astype(jnp.float32)
        if x == 0:
            gain_ref[...] = column(extra[3:4] + extra[4:5] + extra[5:6])
        squares = extra[0:1] + extra[1:2] + extra[2:3]
        scale = lax.rsqrt(squares / features + 1e-05)
        gains = gain_ref[pl.ds(pl.multiple_of(zl_ref[0] * per, per), per), :]
        normed = (picked * scale * gains).astype(jnp.bfloat16)
        right = jnp.concatenate([in_ref[x, z, :toks] for z in range(n_zl)], axis=1)
        total = total + jnp.dot(normed, right, preferred_element_type=jnp.float32)
        out_ref[x] = right
        table = jnp.zeros((AUX // 2, LANES), jnp.float32) + scale
        scale_ref[:, x * LANES : (x + 1) * LANES] = table
    count, few, _ = union_ref.shape
    for i in range(count):
        union_ref[i] = total[i * few : (i + 1) * few]


def sum_spread(groups, in_ref, out_ref):
    count = in_ref.shape[0]
    rest = count // groups
    few = in_ref.shape[1]
    for j in range(rest):
        total = in_ref[j].astype(jnp.float32)
        for i in range(1, groups):
            total = total + in_ref[i * rest + j].astype(jnp.float32)
        total = total.astype(jnp.bfloat16)
        for to in range(out_ref.shape[0]):
            out_ref[to, j * few : (j + 1) * few] = total


def multiply(x_ref, core_ref, gain_in, scale_in, right_in, *refs):
    lefts, refs = refs[:-10], refs[-10:]
    own_out, other_out, gain_ref, scale_ref, right_ref, left_ref, total_ref, half_ref, in_sems, out_sems = refs
    n_x, n_y = len(lefts), own_out.shape[0]
    toks, width = lefts[0].shape
    tile = width // n_y
    pairs = [(gain_in, gain_ref), (scale_in, scale_ref), (right_in, right_ref)]
    pairs += [(left, left_ref.at[j]) for j, left in enumerate(lefts)]
    copies = [pltpu.make_async_copy(a, b, in_sems.at[i]) for i, (a, b) in enumerate(pairs)]
    for copy in copies:
        copy.start()
    for copy in copies:
        copy.wait()
    columns, right = [], []
    for j in range(n_x):
        x = lax.rem(x_ref[0] + n_x - j, n_x)
        row = scale_ref[:1, pl.ds(pl.multiple_of(x * LANES, LANES), LANES)]
        columns.append(jnp.concatenate([column(row)] * (tile // LANES), axis=1))
        right.append(right_ref[x])
    right = jnp.concatenate(right, axis=0)
    rows = tile // 2
    own_rows = pl.ds(pl.multiple_of(core_ref[0] * rows, rows), rows)
    other_rows = pl.ds(pl.multiple_of((1 - core_ref[0]) * rows, rows), rows)
    sent = []
    for y in range(n_y):
        at, slot = slice(y * tile, (y + 1) * tile), y % 2
        normed = []
        for j in range(n_x):
            left = left_ref[j, :, at].astype(jnp.float32) * columns[j] * gain_ref[:, at]
            normed.append(left.astype(jnp.bfloat16))
        if y >= 2:
            for copy in sent[y - 2]:
                copy.wait()
        total_ref[slot] = lax.dot_general(
            jnp.concatenate(normed, axis=0),
            right,
            (((0,), (0,)), ((), ())),
            preferred_element_type=jnp.float32,
        )
        half_ref[slot] = total_ref[slot, other_rows, :].astype(jnp.bfloat16)
        sent.append(
            (
                pltpu.make_async_copy(total_ref.at[slot, own_rows], own_out.at[y], out_sems.at[slot, 0]),
                pltpu.make_async_copy(half_ref.at[slot], other_out.at[y], out_sems.at[slot, 1]),
            )
        )
        for copy in sent[y]:
            copy.start()
    for pair in sent[-2:]:
        for copy in pair:
            copy.wait()


def add_cores(own_ref, got_ref, union_ref, out_ref):
    n_y, n_x, rows, _ = out_ref.shape
    rows -= union_ref.shape[1]
    for y in range(n_y):
        for x in range(n_x):
            at = slice(x * rows, (x + 1) * rows)
            out_ref[y, x, :rows] = (own_ref[y, at] + got_ref[y, at].astype(jnp.float32)).astype(jnp.bfloat16)
            out_ref[y, x, rows:] = union_ref[0]


def add_y(in_ref, out_ref, union_ref):
    n_y, n_x, _, _ = in_ref.shape
    n_zh, _, rows, _ = out_ref.shape
    for x in range(n_x):
        for z in range(n_zh):
            at = slice(z * rows, (z + 1) * rows)
            total = in_ref[0, x, at].astype(jnp.float32)
            for y in range(1, n_y):
                total = total + in_ref[y, x, at].astype(jnp.float32)
            out_ref[z, x] = total.astype(jnp.bfloat16)
        for y in range(n_y):
            union_ref[y, x] = in_ref[y, x, n_zh * rows :]


def finish(first_ref, ids_ref, in_ref, key_ref, value_ref):
    n_zh, n_x, rows, cols = in_ref.shape
    row = lax.broadcasted_iota(jnp.int32, (rows, LANES), 0) + first_ref[0]
    hits = jnp.sum(jnp.where(row == ids_ref[...], 1.0, 0.0), axis=1, keepdims=True)
    for x in range(n_x):
        total = in_ref[0, x].astype(jnp.float32)
        for z in range(1, n_zh):
            total = total + in_ref[z, x].astype(jnp.float32)
        total = jnp.where(hits > 0.0, 0.0, total)
        out_ref = value_ref if x // 2 else key_ref
        for z in range(cols // LANES):
            at = LANES * (2 * z + x % 2)
            out_ref[0, :, at : at + LANES] = total[:, z * LANES : (z + 1) * LANES]


def lay_out(n_zl, core_ref, own_ref, got_ref, key_ref, value_ref):
    n_y, n_x, rows, cols = own_ref.shape
    few = rows // n_zl
    per = key_ref.shape[0] // n_zl
    first = core_ref[0] == 0
    for x in range(n_x):
        out_ref = value_ref if x // 2 else key_ref
        blocks = []
        for y in range(n_y):
            own, got = own_ref[y, x].astype(jnp.float32), got_ref[y, x].astype(jnp.float32)
            blocks += [jnp.where(first, own, got), jnp.where(first, got, own)]
        for z in range(n_zl):
            lines = jnp.concatenate([block[few * z : few * (z + 1)] for block in blocks], axis=0)
            for j in range(cols // LANES):
                at = LANES * (2 * j + x % 2)
                out_ref[per * z : per * (z + 1), at : at + LANES] = lines[:, j * LANES : (j + 1) * LANES]


def call(body, out_shape, args, scalars=0, scratch=(), cost=0):
    single = not isinstance(out_shape, tuple)
    return pl.pallas_call(
        body,
        out_shape=out_shape,
        in_specs=[SMEM] * scalars + [VMEM] * (len(args) - scalars),
        out_specs=VMEM if single else tuple(VMEM for _ in out_shape),
        scratch_shapes=scratch,
        cost_estimate=pl.CostEstimate(flops=0, bytes_accessed=cost, transcendentals=0) if cost else None,
        compiler_params=PARAMS,
    )(*args)


def exchange(v, axes):
    return lax.all_to_all(v, axes, split_axis=0, concat_axis=0, tiled=True)


def shift(v, axis, by):
    count = lax.axis_size(axis)
    return lax.ppermute(v, axis, [(i, (i + by) % count) for i in range(count)])


def per_device(hidden_in, norm_gain, key_cotangent, value_cotangent, union_ids):
    bf16, f32 = jnp.bfloat16, jnp.float32
    toks, width = hidden_in.shape
    n_y, n_core, n_x, n_zh, n_zl = (lax.axis_size(a) for a in AXES)
    y, core, x, zh, zl = (lax.axis_index(a).astype(jnp.int32) for a in AXES)
    n_union = union_ids.shape[0]
    heads = key_cotangent.shape[1] * n_zl
    cols = n_zl * LANES
    per = n_union // n_zl
    shape = jax.ShapeDtypeStruct
    ids = union_ids.reshape(1, n_union)
    gain = norm_gain.reshape(1, width)
    at_y, at_x, at_core, at_zl = (v.reshape(1) for v in (y, x, core, zl))

    inputs = (hidden_in, key_cotangent, value_cotangent, ids, gain)
    packed = pl.pallas_call(
        prepare,
        out_shape=shape((n_x, n_zl, toks + per + AUX, LANES), bf16),
        in_specs=[SMEM] + [pl.BlockSpec(memory_space=pl.ANY)] * len(inputs),
        out_specs=VMEM,
        scratch_shapes=[pltpu.VMEM(v.shape, v.dtype) for v in inputs]
        + [pltpu.SemaphoreType.DMA((len(inputs),))],
        compiler_params=pltpu.CompilerParams(vmem_limit_bytes=60 * 1024 * 1024),
    )(at_zl, *inputs)
    packed = exchange(packed.reshape((n_x * n_zl,) + packed.shape[2:]), ("x", "zl"))
    few = per // (n_y * n_core)
    right, scale, outliers = call(
        lambda *refs: unpack(float(width * n_zl), *refs),
        (
            shape((n_x, toks, cols), bf16),
            shape((AUX // 2, n_x * LANES), f32),
            shape((n_y * n_core, few, cols), f32),
        ),
        (at_zl, packed.reshape((n_x, n_zl) + packed.shape[1:])),
        1,
        [pltpu.VMEM((LANES, LANES), f32)],
    )
    left = [hidden_in] + [shift(hidden_in, "x", k) for k in range(1, n_x)]

    outliers = exchange(outliers, ("y", "core"))
    outliers = call(
        lambda *refs: sum_spread(n_y * n_core, *refs),
        shape((n_zh * n_zl, few, cols), bf16),
        (outliers,),
    )
    outliers = exchange(outliers, ("zh", "zl"))
    outliers = call(
        lambda *refs: sum_spread(n_zh, *refs),
        shape((1, n_zl * few, cols), bf16),
        (outliers,),
    )

    half = shape((n_y, width // (n_y * n_core), cols), f32)
    anywhere = pl.BlockSpec(memory_space=pl.ANY)
    own, other = pl.pallas_call(
        multiply,
        out_shape=(half, shape(half.shape, bf16)),
        in_specs=[SMEM, SMEM] + [anywhere] * (3 + n_x),
        out_specs=(anywhere, anywhere),
        scratch_shapes=[
            pltpu.VMEM(gain.shape, f32),
            pltpu.VMEM(scale.shape, f32),
            pltpu.VMEM(right.shape, bf16),
            pltpu.VMEM((n_x, toks, width), bf16),
            pltpu.VMEM((2, width // n_y, cols), f32),
            pltpu.VMEM((2, width // (n_y * n_core), cols), bf16),
            pltpu.SemaphoreType.DMA((3 + n_x,)),
            pltpu.SemaphoreType.DMA((2, 2)),
        ],
        cost_estimate=pl.CostEstimate(flops=0, bytes_accessed=128 * 1024 * 1024, transcendentals=0),
        compiler_params=pltpu.CompilerParams(vmem_limit_bytes=60 * 1024 * 1024),
    )(at_x, at_core, gain, scale, right, *left)
    other, outliers = lax.optimization_barrier((other, outliers))
    got = shift(other, "core", 1)
    rows = width // (n_y * n_core * n_x * n_zh)
    lines = n_zh * rows + n_zl * few
    pieces = call(add_cores, shape((n_y, n_x, lines, cols), bf16), (own, got, outliers))
    pieces = exchange(pieces.reshape(n_y * n_x, lines, cols), ("y", "x"))
    pieces, outliers = call(
        add_y,
        (shape((n_zh, n_x, rows, cols), bf16), shape((n_y, n_x, n_zl * few, cols), bf16)),
        (pieces.reshape(n_y, n_x, lines, cols),),
    )
    union = shape((n_union, heads), f32)
    union_key, union_value = call(
        lambda *refs: lay_out(n_zl, *refs),
        (union, union),
        (at_core, outliers, shift(outliers, "core", 1)),
        1,
    )
    pieces = exchange(pieces, "zh")
    first = zl * width + rows * (((y * n_core + core) * n_x + x) * n_zh + zh)
    grad = shape((1, rows, heads), f32)
    grad_key, grad_value = call(finish, (grad, grad), (first.reshape(1), ids, pieces), 1)
    return (grad_key, grad_value, union_key, union_value)


def solution(mesh):
    sizes = dict(mesh.shape)
    split = Mesh(
        mesh.devices.reshape(sizes["group"] // 2, 2, 4, sizes["loop"] // 4, sizes["mp"]), AXES
    )
    rows = ("y", "core", "x", "zh")
    return jax.shard_map(
        per_device,
        mesh=split,
        in_specs=(P(rows, "zl"), P("zl"), P(rows, "zl"), P(rows, "zl"), P()),
        out_specs=(P("zl", rows, None), P("zl", rows, None), P(), P()),
        check_vma=False,
    )
```

```python
import jax
import jax.numpy as jnp
from jax import lax
from jax.experimental import pallas as pl
from jax.experimental.pallas import tpu as pltpu
from jax.sharding import Mesh, PartitionSpec as P

AXES = ("y", "core", "x", "zh", "zl")
LANES = 128
AUX = 16
VMEM = pl.BlockSpec(memory_space=pltpu.VMEM)
SMEM = pl.BlockSpec(memory_space=pltpu.SMEM)
PARAMS = pltpu.CompilerParams(vmem_limit_bytes=20 * 1024 * 1024)


def split3(v):
    hi = v.astype(jnp.bfloat16).astype(jnp.float32)
    mid = (v - hi).astype(jnp.bfloat16).astype(jnp.float32)
    low = (v - hi - mid).astype(jnp.bfloat16).astype(jnp.float32)
    return hi, mid, low


def column(row):
    return jnp.broadcast_to(row, (LANES, LANES)).T


def prepare(zl_ref, hidden_in, key_in, value_in, ids_in, gain_in, *refs):
    packed_ref, hidden_ref, key_ref, value_ref, ids_ref, gain_ref, sems = refs
    copies = [
        pltpu.make_async_copy(source, target, sems.at[i])
        for i, (source, target) in enumerate(
            [
                (hidden_in, hidden_ref),
                (key_in, key_ref),
                (value_in, value_ref),
                (ids_in, ids_ref),
                (gain_in, gain_ref),
            ]
        )
    ]
    for copy in copies:
        copy.start()
    n_x, n_zl, _, _ = packed_ref.shape
    toks, width = hidden_ref.shape
    n_union = ids_ref.shape[1]
    per = n_union // n_zl
    for copy in copies[1:]:
        copy.wait()
    for x in range(n_x):
        source = key_ref if x < n_x // 2 else value_ref
        at = LANES * (x % (n_x // 2))
        for z in range(n_zl):
            packed_ref[x, z, :toks] = source[:, at : at + LANES]
    ids = column(ids_ref[...].astype(jnp.float32))[:, :1].astype(jnp.int32) - zl_ref[0] * width
    hit = lax.broadcasted_iota(jnp.int32, (n_union, width), 1) == ids
    gains = jnp.sum(jnp.where(hit, gain_ref[...], 0.0), axis=1, keepdims=True)
    copies[0].wait()
    hidden = hidden_ref[...]
    hidden_f = hidden.astype(jnp.float32)
    squares = jnp.sum(hidden_f * hidden_f, axis=1, keepdims=True)
    picked = lax.dot_general(
        jnp.where(hit, 1.0, 0.0).astype(jnp.bfloat16),
        hidden,
        (((1,), (1,)), ((), ())),
        preferred_element_type=jnp.float32,
    ).astype(jnp.bfloat16)
    lane = lax.broadcasted_iota(jnp.int32, (toks, LANES), 1)
    table = jnp.zeros((toks, LANES), jnp.float32)
    for place, part in enumerate(split3(squares) + split3(gains)):
        table = jnp.where(lane == place, part, table)
    extra = table.T[:AUX].astype(jnp.bfloat16)
    for x in range(n_x):
        for z in range(n_zl):
            packed_ref[x, z, toks : toks + per] = picked[per * z : per * (z + 1)]
            packed_ref[x, z, toks + per :] = extra


def unpack(features, zl_ref, in_ref, out_ref, scale_ref, union_ref, gain_ref):
    n_x, n_zl, rows, _ = in_ref.shape
    toks = LANES
    per = rows - toks - AUX
    total = jnp.zeros((per, n_zl * LANES), jnp.float32)
    for x in range(n_x):
        extra = in_ref[x, 0, toks + per :].astype(jnp.float32)
        picked = in_ref[x, 0, toks : toks + per].astype(jnp.float32)
        for z in range(1, n_zl):
            extra = extra + in_ref[x, z, toks + per :].astype(jnp.float32)
            picked = picked + in_ref[x, z, toks : toks + per].astype(jnp.float32)
        if x == 0:
            gain_ref[...] = column(extra[3:4] + extra[4:5] + extra[5:6])
        squares = extra[0:1] + extra[1:2] + extra[2:3]
        scale = lax.rsqrt(squares / features + 1e-05)
        gains = gain_ref[pl.ds(pl.multiple_of(zl_ref[0] * per, per), per), :]
        normed = (picked * scale * gains).astype(jnp.bfloat16)
        right = jnp.concatenate([in_ref[x, z, :toks] for z in range(n_zl)], axis=1)
        total = total + jnp.dot(normed, right, preferred_element_type=jnp.float32)
        out_ref[x] = right
        table = jnp.zeros((AUX // 2, LANES), jnp.float32) + scale
        scale_ref[:, x * LANES : (x + 1) * LANES] = table
    count, few, _ = union_ref.shape
    for i in range(count):
        union_ref[i] = total[i * few : (i + 1) * few]


def sum_spread(groups, in_ref, out_ref):
    count = in_ref.shape[0]
    rest = count // groups
    few = in_ref.shape[1]
    for j in range(rest):
        total = in_ref[j].astype(jnp.float32)
        for i in range(1, groups):
            total = total + in_ref[i * rest + j].astype(jnp.float32)
        total = total.astype(jnp.bfloat16)
        for to in range(out_ref.shape[0]):
            out_ref[to, j * few : (j + 1) * few] = total


def multiply(x_ref, core_ref, gain_in, scale_in, right_in, *refs):
    lefts, refs = refs[:-10], refs[-10:]
    own_out, other_out, gain_ref, scale_ref, right_ref, left_ref, total_ref, half_ref, in_sems, out_sems = refs
    n_x, n_y = len(lefts), own_out.shape[0]
    toks, width = lefts[0].shape
    tile = width // n_y
    pairs = [(gain_in, gain_ref), (scale_in, scale_ref), (right_in, right_ref)]
    copies = [pltpu.make_async_copy(a, b, in_sems.at[n_y, i]) for i, (a, b) in enumerate(pairs)]
    quarters = []
    for y in range(n_y):
        at = pl.ds(y * tile, tile)
        quarters.append(
            [
                pltpu.make_async_copy(left.at[:, at], left_ref.at[j, :, at], in_sems.at[y, j])
                for j, left in enumerate(lefts)
            ]
        )
    for copy in copies + sum(quarters, []):
        copy.start()
    for copy in copies:
        copy.wait()
    columns, right = [], []
    for j in range(n_x):
        x = lax.rem(x_ref[0] + n_x - j, n_x)
        row = scale_ref[:1, pl.ds(pl.multiple_of(x * LANES, LANES), LANES)]
        columns.append(jnp.concatenate([column(row)] * (tile // LANES), axis=1))
        right.append(right_ref[x])
    right = jnp.concatenate(right, axis=0)
    rows = tile // 2
    own_rows = pl.ds(pl.multiple_of(core_ref[0] * rows, rows), rows)
    other_rows = pl.ds(pl.multiple_of((1 - core_ref[0]) * rows, rows), rows)
    sent = []
    for y in range(n_y):
        at, slot = slice(y * tile, (y + 1) * tile), y % 2
        for copy in quarters[y]:
            copy.wait()
        normed = []
        for j in range(n_x):
            left = left_ref[j, :, at].astype(jnp.float32) * columns[j] * gain_ref[:, at]
            normed.append(left.astype(jnp.bfloat16))
        if y >= 2:
            for copy in sent[y - 2]:
                copy.wait()
        total_ref[slot] = lax.dot_general(
            jnp.concatenate(normed, axis=0),
            right,
            (((0,), (0,)), ((), ())),
            preferred_element_type=jnp.float32,
        )
        half_ref[slot] = total_ref[slot, other_rows, :].astype(jnp.bfloat16)
        sent.append(
            (
                pltpu.make_async_copy(total_ref.at[slot, own_rows], own_out.at[y], out_sems.at[slot, 0]),
                pltpu.make_async_copy(half_ref.at[slot], other_out.at[y], out_sems.at[slot, 1]),
            )
        )
        for copy in sent[y]:
            copy.start()
    for pair in sent[-2:]:
        for copy in pair:
            copy.wait()


def fetch(source, out_ref, sems):
    count = out_ref.shape[0]
    copies = [pltpu.make_async_copy(source.at[y], out_ref.at[y], sems.at[y]) for y in range(count)]
    for copy in copies:
        copy.start()
    for copy in copies:
        copy.wait()


def add_cores(own_ref, got_ref, union_ref, out_ref):
    n_y, n_x, rows, _ = out_ref.shape
    rows -= union_ref.shape[1]
    for y in range(n_y):
        for x in range(n_x):
            at = slice(x * rows, (x + 1) * rows)
            out_ref[y, x, :rows] = (own_ref[y, at] + got_ref[y, at].astype(jnp.float32)).astype(jnp.bfloat16)
            out_ref[y, x, rows:] = union_ref[0]


def add_y(in_ref, out_ref, union_ref):
    n_y, n_x, _, _ = in_ref.shape
    n_zh, _, rows, _ = out_ref.shape
    for x in range(n_x):
        for z in range(n_zh):
            at = slice(z * rows, (z + 1) * rows)
            total = in_ref[0, x, at].astype(jnp.float32)
            for y in range(1, n_y):
                total = total + in_ref[y, x, at].astype(jnp.float32)
            out_ref[z, x] = total.astype(jnp.bfloat16)
        for y in range(n_y):
            union_ref[y, x] = in_ref[y, x, n_zh * rows :]


def finish(first_ref, ids_ref, in_ref, key_ref, value_ref):
    n_zh, n_x, rows, cols = in_ref.shape
    row = lax.broadcasted_iota(jnp.int32, (rows, LANES), 0) + first_ref[0]
    hits = jnp.sum(jnp.where(row == ids_ref[...], 1.0, 0.0), axis=1, keepdims=True)
    for x in range(n_x):
        total = in_ref[0, x].astype(jnp.float32)
        for z in range(1, n_zh):
            total = total + in_ref[z, x].astype(jnp.float32)
        total = jnp.where(hits > 0.0, 0.0, total)
        out_ref = value_ref if x // 2 else key_ref
        for z in range(cols // LANES):
            at = LANES * (2 * z + x % 2)
            out_ref[0, :, at : at + LANES] = total[:, z * LANES : (z + 1) * LANES]


def lay_out(n_zl, core_ref, own_ref, got_ref, key_ref, value_ref):
    n_y, n_x, rows, cols = own_ref.shape
    few = rows // n_zl
    per = key_ref.shape[0] // n_zl
    first = core_ref[0] == 0
    for x in range(n_x):
        out_ref = value_ref if x // 2 else key_ref
        blocks = []
        for y in range(n_y):
            own, got = own_ref[y, x].astype(jnp.float32), got_ref[y, x].astype(jnp.float32)
            blocks += [jnp.where(first, own, got), jnp.where(first, got, own)]
        for z in range(n_zl):
            lines = jnp.concatenate([block[few * z : few * (z + 1)] for block in blocks], axis=0)
            for j in range(cols // LANES):
                at = LANES * (2 * j + x % 2)
                out_ref[per * z : per * (z + 1), at : at + LANES] = lines[:, j * LANES : (j + 1) * LANES]


def call(body, out_shape, args, scalars=0, scratch=(), cost=0):
    single = not isinstance(out_shape, tuple)
    return pl.pallas_call(
        body,
        out_shape=out_shape,
        in_specs=[SMEM] * scalars + [VMEM] * (len(args) - scalars),
        out_specs=VMEM if single else tuple(VMEM for _ in out_shape),
        scratch_shapes=scratch,
        cost_estimate=pl.CostEstimate(flops=0, bytes_accessed=cost, transcendentals=0) if cost else None,
        compiler_params=PARAMS,
    )(*args)


def exchange(v, axes):
    return lax.all_to_all(v, axes, split_axis=0, concat_axis=0, tiled=True)


def shift(v, axis, by):
    count = lax.axis_size(axis)
    return lax.ppermute(v, axis, [(i, (i + by) % count) for i in range(count)])


def per_device(hidden_in, norm_gain, key_cotangent, value_cotangent, union_ids):
    bf16, f32 = jnp.bfloat16, jnp.float32
    toks, width = hidden_in.shape
    n_y, n_core, n_x, n_zh, n_zl = (lax.axis_size(a) for a in AXES)
    y, core, x, zh, zl = (lax.axis_index(a).astype(jnp.int32) for a in AXES)
    n_union = union_ids.shape[0]
    heads = key_cotangent.shape[1] * n_zl
    cols = n_zl * LANES
    per = n_union // n_zl
    shape = jax.ShapeDtypeStruct
    ids = union_ids.reshape(1, n_union)
    gain = norm_gain.reshape(1, width)
    at_y, at_x, at_core, at_zl = (v.reshape(1) for v in (y, x, core, zl))

    inputs = (hidden_in, key_cotangent, value_cotangent, ids, gain)
    packed = pl.pallas_call(
        prepare,
        out_shape=shape((n_x, n_zl, toks + per + AUX, LANES), bf16),
        in_specs=[SMEM] + [pl.BlockSpec(memory_space=pl.ANY)] * len(inputs),
        out_specs=VMEM,
        scratch_shapes=[pltpu.VMEM(v.shape, v.dtype) for v in inputs]
        + [pltpu.SemaphoreType.DMA((len(inputs),))],
        compiler_params=pltpu.CompilerParams(vmem_limit_bytes=60 * 1024 * 1024),
    )(at_zl, *inputs)
    packed = exchange(packed.reshape((n_x * n_zl,) + packed.shape[2:]), ("x", "zl"))
    few = per // (n_y * n_core)
    right, scale, outliers = call(
        lambda *refs: unpack(float(width * n_zl), *refs),
        (
            shape((n_x, toks, cols), bf16),
            shape((AUX // 2, n_x * LANES), f32),
            shape((n_y * n_core, few, cols), f32),
        ),
        (at_zl, packed.reshape((n_x, n_zl) + packed.shape[1:])),
        1,
        [pltpu.VMEM((LANES, LANES), f32)],
    )
    left = [hidden_in] + [shift(hidden_in, "x", k) for k in range(1, n_x)]

    outliers = exchange(outliers, ("y", "core"))
    outliers = call(
        lambda *refs: sum_spread(n_y * n_core, *refs),
        shape((n_zh * n_zl, few, cols), bf16),
        (outliers,),
    )
    outliers = exchange(outliers, ("zh", "zl"))
    outliers = call(
        lambda *refs: sum_spread(n_zh, *refs),
        shape((1, n_zl * few, cols), bf16),
        (outliers,),
    )

    half = shape((n_y, width // (n_y * n_core), cols), f32)
    anywhere = pl.BlockSpec(memory_space=pl.ANY)
    own, other = pl.pallas_call(
        multiply,
        out_shape=(half, shape(half.shape, bf16)),
        in_specs=[SMEM, SMEM] + [anywhere] * (3 + n_x),
        out_specs=(anywhere, anywhere),
        scratch_shapes=[
            pltpu.VMEM(gain.shape, f32),
            pltpu.VMEM(scale.shape, f32),
            pltpu.VMEM(right.shape, bf16),
            pltpu.VMEM((n_x, toks, width), bf16),
            pltpu.VMEM((2, width // n_y, cols), f32),
            pltpu.VMEM((2, width // (n_y * n_core), cols), bf16),
            pltpu.SemaphoreType.DMA((n_y + 1, n_x)),
            pltpu.SemaphoreType.DMA((2, 2)),
        ],
        cost_estimate=pl.CostEstimate(flops=0, bytes_accessed=128 * 1024 * 1024, transcendentals=0),
        compiler_params=pltpu.CompilerParams(vmem_limit_bytes=60 * 1024 * 1024),
    )(at_x, at_core, gain, scale, right, *left)
    other, outliers = lax.optimization_barrier((other, outliers))
    got = shift(other, "core", 1)
    own = pl.pallas_call(
        fetch,
        out_shape=half,
        in_specs=[anywhere],
        out_specs=VMEM,
        scratch_shapes=[pltpu.SemaphoreType.DMA((n_y,))],
        cost_estimate=pl.CostEstimate(flops=0, bytes_accessed=16 * 1024 * 1024, transcendentals=0),
        compiler_params=PARAMS,
    )(own)
    rows = width // (n_y * n_core * n_x * n_zh)
    lines = n_zh * rows + n_zl * few
    pieces = call(add_cores, shape((n_y, n_x, lines, cols), bf16), (own, got, outliers))
    pieces = exchange(pieces.reshape(n_y * n_x, lines, cols), ("y", "x"))
    pieces, outliers = call(
        add_y,
        (shape((n_zh, n_x, rows, cols), bf16), shape((n_y, n_x, n_zl * few, cols), bf16)),
        (pieces.reshape(n_y, n_x, lines, cols),),
    )
    union = shape((n_union, heads), f32)
    union_key, union_value = call(
        lambda *refs: lay_out(n_zl, *refs),
        (union, union),
        (at_core, outliers, shift(outliers, "core", 1)),
        1,
    )
    pieces = exchange(pieces, "zh")
    first = zl * width + rows * (((y * n_core + core) * n_x + x) * n_zh + zh)
    grad = shape((1, rows, heads), f32)
    grad_key, grad_value = call(finish, (grad, grad), (first.reshape(1), ids, pieces), 1)
    return (grad_key, grad_value, union_key, union_value)


def solution(mesh):
    sizes = dict(mesh.shape)
    split = Mesh(
        mesh.devices.reshape(sizes["group"] // 2, 2, 4, sizes["loop"] // 4, sizes["mp"]), AXES
    )
    rows = ("y", "core", "x", "zh")
    return jax.shard_map(
        per_device,
        mesh=split,
        in_specs=(P(rows, "zl"), P("zl"), P(rows, "zl"), P(rows, "zl"), P()),
        out_specs=(P("zl", rows, None), P("zl", rows, None), P(), P()),
        check_vma=False,
    )
```

```python
import jax
import jax.numpy as jnp
from jax import lax
from jax.experimental import pallas as pl
from jax.experimental.pallas import tpu as pltpu
from jax.sharding import Mesh, PartitionSpec as P

AXES = ("y", "core", "x", "zh", "zl")
LANES = 128
AUX = 8
VMEM = pl.BlockSpec(memory_space=pltpu.VMEM)
SMEM = pl.BlockSpec(memory_space=pltpu.SMEM)
PARAMS = pltpu.CompilerParams(vmem_limit_bytes=20 * 1024 * 1024)


def split3(v):
    hi = v.astype(jnp.bfloat16).astype(jnp.float32)
    mid = (v - hi).astype(jnp.bfloat16).astype(jnp.float32)
    low = (v - hi - mid).astype(jnp.bfloat16).astype(jnp.float32)
    return hi, mid, low


def column(row):
    return jnp.broadcast_to(row, (LANES, LANES)).T


def prepare(zl_ref, hidden_in, key_in, value_in, ids_in, gain_in, *refs):
    packed_ref, hidden_ref, key_ref, value_ref, ids_ref, gain_ref, sems = refs
    copies = [
        pltpu.make_async_copy(source, target, sems.at[i])
        for i, (source, target) in enumerate(
            [
                (hidden_in, hidden_ref),
                (key_in, key_ref),
                (value_in, value_ref),
                (ids_in, ids_ref),
                (gain_in, gain_ref),
            ]
        )
    ]
    for copy in copies:
        copy.start()
    n_x, n_zl, _, _ = packed_ref.shape
    toks, width = hidden_ref.shape
    n_union = ids_ref.shape[1]
    per = n_union // n_zl
    for copy in copies[1:]:
        copy.wait()
    for x in range(n_x):
        source = key_ref if x < n_x // 2 else value_ref
        at = LANES * (x % (n_x // 2))
        for z in range(n_zl):
            packed_ref[x, z, :toks] = source[:, at : at + LANES]
    ids = column(ids_ref[...].astype(jnp.float32))[:, :1].astype(jnp.int32) - zl_ref[0] * width
    hit = lax.broadcasted_iota(jnp.int32, (n_union, width), 1) == ids
    gains = jnp.sum(jnp.where(hit, gain_ref[...], 0.0), axis=1, keepdims=True)
    copies[0].wait()
    hidden = hidden_ref[...]
    both = lax.dot_general(
        jnp.concatenate([jnp.where(hit, 1.0, 0.0).astype(jnp.bfloat16), hidden], axis=0),
        hidden,
        (((1,), (1,)), ((), ())),
        preferred_element_type=jnp.float32,
    )
    picked = both[:n_union].astype(jnp.bfloat16)
    row = lax.broadcasted_iota(jnp.int32, (toks, LANES), 0)
    lane = lax.broadcasted_iota(jnp.int32, (toks, LANES), 1)
    squares = jnp.sum(jnp.where(row == lane, both[n_union:], 0.0), axis=0, keepdims=True)
    gains = jnp.broadcast_to(gains, (n_union, LANES)).T[:1]
    table = jnp.zeros((AUX, LANES), jnp.float32)
    for place, part in enumerate(split3(squares) + split3(gains)):
        table = jnp.where(row[:AUX] == place, part, table)
    extra = table.astype(jnp.bfloat16)
    for x in range(n_x):
        for z in range(n_zl):
            packed_ref[x, z, toks : toks + per] = picked[per * z : per * (z + 1)]
            packed_ref[x, z, toks + per :] = extra


def unpack(features, zl_ref, in_ref, out_ref, scale_ref, union_ref, gain_ref):
    n_x, n_zl, rows, _ = in_ref.shape
    toks = LANES
    per = rows - toks - AUX
    total = jnp.zeros((per, n_zl * LANES), jnp.float32)
    for x in range(n_x):
        extra = in_ref[x, 0, toks + per :].astype(jnp.float32)
        picked = in_ref[x, 0, toks : toks + per].astype(jnp.float32)
        for z in range(1, n_zl):
            extra = extra + in_ref[x, z, toks + per :].astype(jnp.float32)
            picked = picked + in_ref[x, z, toks : toks + per].astype(jnp.float32)
        if x == 0:
            gain_ref[...] = column(extra[3:4] + extra[4:5] + extra[5:6])
        squares = extra[0:1] + extra[1:2] + extra[2:3]
        scale = lax.rsqrt(squares / features + 1e-05)
        gains = gain_ref[pl.ds(pl.multiple_of(zl_ref[0] * per, per), per), :]
        normed = (picked * scale * gains).astype(jnp.bfloat16)
        right = jnp.concatenate([in_ref[x, z, :toks] for z in range(n_zl)], axis=1)
        total = total + jnp.dot(normed, right, preferred_element_type=jnp.float32)
        out_ref[x] = right
        table = jnp.zeros((AUX, LANES), jnp.float32) + scale
        scale_ref[:, x * LANES : (x + 1) * LANES] = table
    count, few, _ = union_ref.shape
    for i in range(count):
        union_ref[i] = total[i * few : (i + 1) * few]


def sum_spread(groups, in_ref, out_ref):
    count = in_ref.shape[0]
    rest = count // groups
    few = in_ref.shape[1]
    for j in range(rest):
        total = in_ref[j].astype(jnp.float32)
        for i in range(1, groups):
            total = total + in_ref[i * rest + j].astype(jnp.float32)
        total = total.astype(jnp.bfloat16)
        for to in range(out_ref.shape[0]):
            out_ref[to, j * few : (j + 1) * few] = total


def multiply(x_ref, core_ref, gain_in, scale_in, right_in, *refs):
    lefts, refs = refs[:-10], refs[-10:]
    own_out, other_out, gain_ref, scale_ref, right_ref, left_ref, total_ref, half_ref, in_sems, out_sems = refs
    n_x, n_y = len(lefts), own_out.shape[0]
    toks, width = lefts[0].shape
    tile = width // n_y
    pairs = [(gain_in, gain_ref), (scale_in, scale_ref), (right_in, right_ref)]
    copies = [pltpu.make_async_copy(a, b, in_sems.at[n_y, i]) for i, (a, b) in enumerate(pairs)]
    quarters = []
    for y in range(n_y):
        at = pl.ds(y * tile, tile)
        quarters.append(
            [
                pltpu.make_async_copy(left.at[:, at], left_ref.at[j, :, at], in_sems.at[y, j])
                for j, left in enumerate(lefts)
            ]
        )
    for copy in copies + sum(quarters, []):
        copy.start()
    for copy in copies:
        copy.wait()
    columns, right = [], []
    for j in range(n_x):
        x = lax.rem(x_ref[0] + n_x - j, n_x)
        row = scale_ref[:1, pl.ds(pl.multiple_of(x * LANES, LANES), LANES)]
        columns.append(jnp.concatenate([column(row)] * (tile // LANES), axis=1))
        right.append(right_ref[x])
    right = jnp.concatenate(right, axis=0)
    rows = tile // 2
    own_rows = pl.ds(pl.multiple_of(core_ref[0] * rows, rows), rows)
    other_rows = pl.ds(pl.multiple_of((1 - core_ref[0]) * rows, rows), rows)
    sent = []
    for y in range(n_y):
        at, slot = slice(y * tile, (y + 1) * tile), y % 2
        for copy in quarters[y]:
            copy.wait()
        normed = []
        for j in range(n_x):
            left = left_ref[j, :, at].astype(jnp.float32) * columns[j] * gain_ref[:, at]
            normed.append(left.astype(jnp.bfloat16))
        if y >= 2:
            for copy in sent[y - 2]:
                copy.wait()
        total_ref[slot] = lax.dot_general(
            jnp.concatenate(normed, axis=0),
            right,
            (((0,), (0,)), ((), ())),
            preferred_element_type=jnp.float32,
        )
        half_ref[slot] = total_ref[slot, other_rows, :].astype(jnp.bfloat16)
        sent.append(
            (
                pltpu.make_async_copy(total_ref.at[slot, own_rows], own_out.at[y], out_sems.at[slot, 0]),
                pltpu.make_async_copy(half_ref.at[slot], other_out.at[y], out_sems.at[slot, 1]),
            )
        )
        for copy in sent[y]:
            copy.start()
    for pair in sent[-2:]:
        for copy in pair:
            copy.wait()


def fetch(source, out_ref, sems):
    count = out_ref.shape[0]
    copies = [pltpu.make_async_copy(source.at[y], out_ref.at[y], sems.at[y]) for y in range(count)]
    for copy in copies:
        copy.start()
    for copy in copies:
        copy.wait()


def add_cores(own_ref, got_ref, union_ref, out_ref):
    n_y, n_x, rows, _ = out_ref.shape
    rows -= union_ref.shape[1]
    for y in range(n_y):
        for x in range(n_x):
            at = slice(x * rows, (x + 1) * rows)
            out_ref[y, x, :rows] = (own_ref[y, at] + got_ref[y, at].astype(jnp.float32)).astype(jnp.bfloat16)
            out_ref[y, x, rows:] = union_ref[0]


def add_y(in_ref, out_ref, union_ref):
    n_y, n_x, _, _ = in_ref.shape
    n_zh, _, rows, _ = out_ref.shape
    for x in range(n_x):
        for z in range(n_zh):
            at = slice(z * rows, (z + 1) * rows)
            total = in_ref[0, x, at].astype(jnp.float32)
            for y in range(1, n_y):
                total = total + in_ref[y, x, at].astype(jnp.float32)
            out_ref[z, x] = total.astype(jnp.bfloat16)
        for y in range(n_y):
            union_ref[y, x] = in_ref[y, x, n_zh * rows :]


def finish(first_ref, ids_ref, in_ref, key_ref, value_ref):
    n_zh, n_x, rows, cols = in_ref.shape
    row = lax.broadcasted_iota(jnp.int32, (rows, LANES), 0) + first_ref[0]
    hits = jnp.sum(jnp.where(row == ids_ref[...], 1.0, 0.0), axis=1, keepdims=True)
    for x in range(n_x):
        total = in_ref[0, x].astype(jnp.float32)
        for z in range(1, n_zh):
            total = total + in_ref[z, x].astype(jnp.float32)
        total = jnp.where(hits > 0.0, 0.0, total)
        out_ref = value_ref if x // 2 else key_ref
        for z in range(cols // LANES):
            at = LANES * (2 * z + x % 2)
            out_ref[0, :, at : at + LANES] = total[:, z * LANES : (z + 1) * LANES]


def lay_out(n_zl, core_ref, own_ref, got_ref, key_ref, value_ref):
    n_y, n_x, rows, cols = own_ref.shape
    few = rows // n_zl
    per = key_ref.shape[0] // n_zl
    first = core_ref[0] == 0
    for x in range(n_x):
        out_ref = value_ref if x // 2 else key_ref
        blocks = []
        for y in range(n_y):
            own, got = own_ref[y, x].astype(jnp.float32), got_ref[y, x].astype(jnp.float32)
            blocks += [jnp.where(first, own, got), jnp.where(first, got, own)]
        for z in range(n_zl):
            lines = jnp.concatenate([block[few * z : few * (z + 1)] for block in blocks], axis=0)
            for j in range(cols // LANES):
                at = LANES * (2 * j + x % 2)
                out_ref[per * z : per * (z + 1), at : at + LANES] = lines[:, j * LANES : (j + 1) * LANES]


def call(body, out_shape, args, scalars=0, scratch=(), cost=0):
    single = not isinstance(out_shape, tuple)
    return pl.pallas_call(
        body,
        out_shape=out_shape,
        in_specs=[SMEM] * scalars + [VMEM] * (len(args) - scalars),
        out_specs=VMEM if single else tuple(VMEM for _ in out_shape),
        scratch_shapes=scratch,
        cost_estimate=pl.CostEstimate(flops=0, bytes_accessed=cost, transcendentals=0) if cost else None,
        compiler_params=PARAMS,
    )(*args)


def exchange(v, axes):
    return lax.all_to_all(v, axes, split_axis=0, concat_axis=0, tiled=True)


def shift(v, axis, by):
    count = lax.axis_size(axis)
    return lax.ppermute(v, axis, [(i, (i + by) % count) for i in range(count)])


def per_device(hidden_in, norm_gain, key_cotangent, value_cotangent, union_ids):
    bf16, f32 = jnp.bfloat16, jnp.float32
    toks, width = hidden_in.shape
    n_y, n_core, n_x, n_zh, n_zl = (lax.axis_size(a) for a in AXES)
    y, core, x, zh, zl = (lax.axis_index(a).astype(jnp.int32) for a in AXES)
    n_union = union_ids.shape[0]
    heads = key_cotangent.shape[1] * n_zl
    cols = n_zl * LANES
    per = n_union // n_zl
    shape = jax.ShapeDtypeStruct
    ids = union_ids.reshape(1, n_union)
    gain = norm_gain.reshape(1, width)
    at_y, at_x, at_core, at_zl = (v.reshape(1) for v in (y, x, core, zl))

    inputs = (hidden_in, key_cotangent, value_cotangent, ids, gain)
    packed = pl.pallas_call(
        prepare,
        out_shape=shape((n_x, n_zl, toks + per + AUX, LANES), bf16),
        in_specs=[SMEM] + [pl.BlockSpec(memory_space=pl.ANY)] * len(inputs),
        out_specs=VMEM,
        scratch_shapes=[pltpu.VMEM(v.shape, v.dtype) for v in inputs]
        + [pltpu.SemaphoreType.DMA((len(inputs),))],
        compiler_params=pltpu.CompilerParams(vmem_limit_bytes=60 * 1024 * 1024),
    )(at_zl, *inputs)
    packed = exchange(packed.reshape((n_x * n_zl,) + packed.shape[2:]), ("x", "zl"))
    few = per // (n_y * n_core)
    right, scale, outliers = call(
        lambda *refs: unpack(float(width * n_zl), *refs),
        (
            shape((n_x, toks, cols), bf16),
            shape((AUX, n_x * LANES), f32),
            shape((n_y * n_core, few, cols), f32),
        ),
        (at_zl, packed.reshape((n_x, n_zl) + packed.shape[1:])),
        1,
        [pltpu.VMEM((LANES, LANES), f32)],
    )
    left = [hidden_in] + [shift(hidden_in, "x", k) for k in range(1, n_x)]

    outliers = exchange(outliers, ("y", "core"))
    outliers = call(
        lambda *refs: sum_spread(n_y * n_core, *refs),
        shape((n_zh * n_zl, few, cols), bf16),
        (outliers,),
    )
    outliers = exchange(outliers, ("zh", "zl"))
    outliers = call(
        lambda *refs: sum_spread(n_zh, *refs),
        shape((1, n_zl * few, cols), bf16),
        (outliers,),
    )

    half = shape((n_y, width // (n_y * n_core), cols), f32)
    anywhere = pl.BlockSpec(memory_space=pl.ANY)
    own, other = pl.pallas_call(
        multiply,
        out_shape=(half, shape(half.shape, bf16)),
        in_specs=[SMEM, SMEM] + [anywhere] * (3 + n_x),
        out_specs=(anywhere, anywhere),
        scratch_shapes=[
            pltpu.VMEM(gain.shape, f32),
            pltpu.VMEM(scale.shape, f32),
            pltpu.VMEM(right.shape, bf16),
            pltpu.VMEM((n_x, toks, width), bf16),
            pltpu.VMEM((2, width // n_y, cols), f32),
            pltpu.VMEM((2, width // (n_y * n_core), cols), bf16),
            pltpu.SemaphoreType.DMA((n_y + 1, n_x)),
            pltpu.SemaphoreType.DMA((2, 2)),
        ],
        cost_estimate=pl.CostEstimate(flops=0, bytes_accessed=128 * 1024 * 1024, transcendentals=0),
        compiler_params=pltpu.CompilerParams(vmem_limit_bytes=60 * 1024 * 1024),
    )(at_x, at_core, gain, scale, right, *left)
    other, outliers = lax.optimization_barrier((other, outliers))
    got = shift(other, "core", 1)
    own = pl.pallas_call(
        fetch,
        out_shape=half,
        in_specs=[anywhere],
        out_specs=VMEM,
        scratch_shapes=[pltpu.SemaphoreType.DMA((n_y,))],
        cost_estimate=pl.CostEstimate(flops=0, bytes_accessed=16 * 1024 * 1024, transcendentals=0),
        compiler_params=PARAMS,
    )(own)
    rows = width // (n_y * n_core * n_x * n_zh)
    lines = n_zh * rows + n_zl * few
    pieces = call(add_cores, shape((n_y, n_x, lines, cols), bf16), (own, got, outliers))
    pieces = exchange(pieces.reshape(n_y * n_x, lines, cols), ("y", "x"))
    pieces, outliers = call(
        add_y,
        (shape((n_zh, n_x, rows, cols), bf16), shape((n_y, n_x, n_zl * few, cols), bf16)),
        (pieces.reshape(n_y, n_x, lines, cols),),
    )
    union = shape((n_union, heads), f32)
    union_key, union_value = call(
        lambda *refs: lay_out(n_zl, *refs),
        (union, union),
        (at_core, outliers, shift(outliers, "core", 1)),
        1,
    )
    pieces = exchange(pieces, "zh")
    first = zl * width + rows * (((y * n_core + core) * n_x + x) * n_zh + zh)
    grad = shape((1, rows, heads), f32)
    grad_key, grad_value = call(finish, (grad, grad), (first.reshape(1), ids, pieces), 1)
    return (grad_key, grad_value, union_key, union_value)


def solution(mesh):
    sizes = dict(mesh.shape)
    split = Mesh(
        mesh.devices.reshape(sizes["group"] // 2, 2, 4, sizes["loop"] // 4, sizes["mp"]), AXES
    )
    rows = ("y", "core", "x", "zh")
    return jax.shard_map(
        per_device,
        mesh=split,
        in_specs=(P(rows, "zl"), P("zl"), P(rows, "zl"), P(rows, "zl"), P()),
        out_specs=(P("zl", rows, None), P("zl", rows, None), P(), P()),
        check_vma=False,
    )
```

```python
import jax
import jax.numpy as jnp
from jax import lax
from jax.experimental import pallas as pl
from jax.experimental.pallas import tpu as pltpu
from jax.sharding import Mesh, PartitionSpec as P

AXES = ("y", "core", "x", "zh", "zl")
LANES = 128
AUX = 8
VMEM = pl.BlockSpec(memory_space=pltpu.VMEM)
SMEM = pl.BlockSpec(memory_space=pltpu.SMEM)
PARAMS = pltpu.CompilerParams(vmem_limit_bytes=20 * 1024 * 1024)


def split3(v):
    hi = v.astype(jnp.bfloat16).astype(jnp.float32)
    mid = (v - hi).astype(jnp.bfloat16).astype(jnp.float32)
    low = (v - hi - mid).astype(jnp.bfloat16).astype(jnp.float32)
    return hi, mid, low


def column(row):
    return jnp.broadcast_to(row, (LANES, LANES)).T


def prepare(zl_ref, hidden_in, key_in, value_in, ids_in, gain_in, *refs):
    packed_ref, hidden_ref, key_ref, value_ref, ids_ref, gain_ref, sems = refs
    copies = [
        pltpu.make_async_copy(source, target, sems.at[i])
        for i, (source, target) in enumerate(
            [
                (hidden_in, hidden_ref),
                (key_in, key_ref),
                (value_in, value_ref),
                (ids_in, ids_ref),
                (gain_in, gain_ref),
            ]
        )
    ]
    for copy in copies:
        copy.start()
    n_x, n_zl, _, _ = packed_ref.shape
    toks, width = hidden_ref.shape
    n_union = ids_ref.shape[1]
    per = n_union // n_zl
    for copy in copies[1:]:
        copy.wait()
    for x in range(n_x):
        source = key_ref if x < n_x // 2 else value_ref
        at = LANES * (x % (n_x // 2))
        for z in range(n_zl):
            packed_ref[x, z, :toks] = source[:, at : at + LANES]
    ids = column(ids_ref[...].astype(jnp.float32))[:, :1].astype(jnp.int32) - zl_ref[0] * width
    hit = lax.broadcasted_iota(jnp.int32, (n_union, width), 1) == ids
    gains = jnp.sum(jnp.where(hit, gain_ref[...], 0.0), axis=1, keepdims=True)
    copies[0].wait()
    hidden = hidden_ref[...]
    both = lax.dot_general(
        jnp.concatenate([jnp.where(hit, 1.0, 0.0).astype(jnp.bfloat16), hidden], axis=0),
        hidden,
        (((1,), (1,)), ((), ())),
        preferred_element_type=jnp.float32,
    )
    picked = both[:n_union].astype(jnp.bfloat16)
    row = lax.broadcasted_iota(jnp.int32, (toks, LANES), 0)
    lane = lax.broadcasted_iota(jnp.int32, (toks, LANES), 1)
    squares = jnp.sum(jnp.where(row == lane, both[n_union:], 0.0), axis=0, keepdims=True)
    gains = jnp.broadcast_to(gains, (n_union, LANES)).T[:1]
    table = jnp.zeros((AUX, LANES), jnp.float32)
    for place, part in enumerate(split3(squares) + split3(gains)):
        table = jnp.where(row[:AUX] == place, part, table)
    extra = table.astype(jnp.bfloat16)
    for x in range(n_x):
        for z in range(n_zl):
            packed_ref[x, z, toks : toks + per] = picked[per * z : per * (z + 1)]
            packed_ref[x, z, toks + per :] = extra


def unpack(features, zl_ref, in_ref, out_ref, scale_ref, union_ref, gain_ref):
    n_x, n_zl, rows, _ = in_ref.shape
    toks = LANES
    per = rows - toks - AUX
    total = jnp.zeros((per, n_zl * LANES), jnp.float32)
    for x in range(n_x):
        extra = in_ref[x, 0, toks + per :].astype(jnp.float32)
        picked = in_ref[x, 0, toks : toks + per].astype(jnp.float32)
        for z in range(1, n_zl):
            extra = extra + in_ref[x, z, toks + per :].astype(jnp.float32)
            picked = picked + in_ref[x, z, toks : toks + per].astype(jnp.float32)
        if x == 0:
            gain_ref[...] = column(extra[3:4] + extra[4:5] + extra[5:6])
        squares = extra[0:1] + extra[1:2] + extra[2:3]
        scale = lax.rsqrt(squares / features + 1e-05)
        gains = gain_ref[pl.ds(pl.multiple_of(zl_ref[0] * per, per), per), :]
        normed = (picked * scale * gains).astype(jnp.bfloat16)
        right = jnp.concatenate([in_ref[x, z, :toks] for z in range(n_zl)], axis=1)
        total = total + jnp.dot(normed, right, preferred_element_type=jnp.float32)
        out_ref[x] = right
        table = jnp.zeros((AUX, LANES), jnp.float32) + scale
        scale_ref[:, x * LANES : (x + 1) * LANES] = table
    count, few, _ = union_ref.shape
    for i in range(count):
        union_ref[i] = total[i * few : (i + 1) * few]


def sum_spread(groups, in_ref, out_ref):
    count = in_ref.shape[0]
    rest = count // groups
    few = in_ref.shape[1]
    for j in range(rest):
        total = in_ref[j].astype(jnp.float32)
        for i in range(1, groups):
            total = total + in_ref[i * rest + j].astype(jnp.float32)
        total = total.astype(jnp.bfloat16)
        for to in range(out_ref.shape[0]):
            out_ref[to, j * few : (j + 1) * few] = total


def sum_last(groups, in_ref, out_ref):
    count = in_ref.shape[0]
    rest = count // groups
    few = in_ref.shape[1]
    for j in range(rest):
        total = in_ref[j * groups].astype(jnp.float32)
        for i in range(1, groups):
            total = total + in_ref[j * groups + i].astype(jnp.float32)
        total = total.astype(jnp.bfloat16)
        for to in range(out_ref.shape[0]):
            out_ref[to, j * few : (j + 1) * few] = total


def multiply(x_ref, core_ref, gain_in, scale_in, right_in, *refs):
    lefts, refs = refs[:-10], refs[-10:]
    own_out, other_out, gain_ref, scale_ref, right_ref, left_ref, total_ref, half_ref, in_sems, out_sems = refs
    n_x, n_y = len(lefts), own_out.shape[0]
    toks, width = lefts[0].shape
    tile = width // n_y
    pairs = [(gain_in, gain_ref), (scale_in, scale_ref), (right_in, right_ref)]
    copies = [pltpu.make_async_copy(a, b, in_sems.at[n_y, i]) for i, (a, b) in enumerate(pairs)]
    quarters = []
    for y in range(n_y):
        at = pl.ds(y * tile, tile)
        quarters.append(
            [
                pltpu.make_async_copy(left.at[:, at], left_ref.at[j, :, at], in_sems.at[y, j])
                for j, left in enumerate(lefts)
            ]
        )
    for copy in copies + sum(quarters, []):
        copy.start()
    for copy in copies:
        copy.wait()
    columns, right = [], []
    for j in range(n_x):
        x = lax.rem(x_ref[0] + n_x - j, n_x)
        row = scale_ref[:1, pl.ds(pl.multiple_of(x * LANES, LANES), LANES)]
        columns.append(jnp.concatenate([column(row)] * (tile // LANES), axis=1))
        right.append(right_ref[x])
    right = jnp.concatenate(right, axis=0)
    rows = tile // 2
    own_rows = pl.ds(pl.multiple_of(core_ref[0] * rows, rows), rows)
    other_rows = pl.ds(pl.multiple_of((1 - core_ref[0]) * rows, rows), rows)
    sent = []
    for y in range(n_y):
        at, slot = slice(y * tile, (y + 1) * tile), y % 2
        for copy in quarters[y]:
            copy.wait()
        normed = []
        for j in range(n_x):
            left = left_ref[j, :, at].astype(jnp.float32) * columns[j] * gain_ref[:, at]
            normed.append(left.astype(jnp.bfloat16))
        if y >= 2:
            for copy in sent[y - 2]:
                copy.wait()
        total_ref[slot] = lax.dot_general(
            jnp.concatenate(normed, axis=0),
            right,
            (((0,), (0,)), ((), ())),
            preferred_element_type=jnp.float32,
        )
        half_ref[slot] = total_ref[slot, other_rows, :].astype(jnp.bfloat16)
        sent.append(
            (
                pltpu.make_async_copy(total_ref.at[slot, own_rows], own_out.at[y], out_sems.at[slot, 0]),
                pltpu.make_async_copy(half_ref.at[slot], other_out.at[y], out_sems.at[slot, 1]),
            )
        )
        for copy in sent[y]:
            copy.start()
    for pair in sent[-2:]:
        for copy in pair:
            copy.wait()


def fetch(source, out_ref, sems):
    count = out_ref.shape[0]
    copies = [pltpu.make_async_copy(source.at[y], out_ref.at[y], sems.at[y]) for y in range(count)]
    for copy in copies:
        copy.start()
    for copy in copies:
        copy.wait()


def add_cores(own_ref, got_ref, union_ref, out_ref):
    n_y, n_x, rows, _ = out_ref.shape
    rows -= union_ref.shape[1]
    for y in range(n_y):
        for x in range(n_x):
            at = slice(x * rows, (x + 1) * rows)
            out_ref[y, x, :rows] = (own_ref[y, at] + got_ref[y, at].astype(jnp.float32)).astype(jnp.bfloat16)
            out_ref[y, x, rows:] = union_ref[0]


def add_y(in_ref, out_ref, union_ref):
    n_y, n_x, _, _ = in_ref.shape
    n_zh, _, rows, _ = out_ref.shape
    for x in range(n_x):
        for z in range(n_zh):
            at = slice(z * rows, (z + 1) * rows)
            total = in_ref[0, x, at].astype(jnp.float32)
            for y in range(1, n_y):
                total = total + in_ref[y, x, at].astype(jnp.float32)
            out_ref[z, x] = total.astype(jnp.bfloat16)
        for y in range(n_y):
            union_ref[y, x] = in_ref[y, x, n_zh * rows :]


def finish(first_ref, ids_ref, in_ref, key_ref, value_ref):
    n_zh, n_x, rows, cols = in_ref.shape
    row = lax.broadcasted_iota(jnp.int32, (rows, LANES), 0) + first_ref[0]
    hits = jnp.sum(jnp.where(row == ids_ref[...], 1.0, 0.0), axis=1, keepdims=True)
    for x in range(n_x):
        total = in_ref[0, x].astype(jnp.float32)
        for z in range(1, n_zh):
            total = total + in_ref[z, x].astype(jnp.float32)
        total = jnp.where(hits > 0.0, 0.0, total)
        out_ref = value_ref if x // 2 else key_ref
        for z in range(cols // LANES):
            at = LANES * (2 * z + x % 2)
            out_ref[0, :, at : at + LANES] = total[:, z * LANES : (z + 1) * LANES]


def lay_out(n_zl, core_ref, own_ref, got_ref, key_ref, value_ref):
    n_y, n_x, rows, cols = own_ref.shape
    few = rows // n_zl
    per = key_ref.shape[0] // n_zl
    first = core_ref[0] == 0
    for x in range(n_x):
        out_ref = value_ref if x // 2 else key_ref
        blocks = []
        for y in range(n_y):
            own, got = own_ref[y, x].astype(jnp.float32), got_ref[y, x].astype(jnp.float32)
            blocks += [jnp.where(first, own, got), jnp.where(first, got, own)]
        for z in range(n_zl):
            lines = jnp.concatenate([block[few * z : few * (z + 1)] for block in blocks], axis=0)
            for j in range(cols // LANES):
                at = LANES * (2 * j + x % 2)
                out_ref[per * z : per * (z + 1), at : at + LANES] = lines[:, j * LANES : (j + 1) * LANES]


def call(body, out_shape, args, scalars=0, scratch=(), cost=0):
    single = not isinstance(out_shape, tuple)
    return pl.pallas_call(
        body,
        out_shape=out_shape,
        in_specs=[SMEM] * scalars + [VMEM] * (len(args) - scalars),
        out_specs=VMEM if single else tuple(VMEM for _ in out_shape),
        scratch_shapes=scratch,
        cost_estimate=pl.CostEstimate(flops=0, bytes_accessed=cost, transcendentals=0) if cost else None,
        compiler_params=PARAMS,
    )(*args)


def exchange(v, axes):
    return lax.all_to_all(v, axes, split_axis=0, concat_axis=0, tiled=True)


def shift(v, axis, by):
    count = lax.axis_size(axis)
    return lax.ppermute(v, axis, [(i, (i + by) % count) for i in range(count)])


def per_device(hidden_in, norm_gain, key_cotangent, value_cotangent, union_ids):
    bf16, f32 = jnp.bfloat16, jnp.float32
    toks, width = hidden_in.shape
    n_y, n_core, n_x, n_zh, n_zl = (lax.axis_size(a) for a in AXES)
    y, core, x, zh, zl = (lax.axis_index(a).astype(jnp.int32) for a in AXES)
    n_union = union_ids.shape[0]
    heads = key_cotangent.shape[1] * n_zl
    cols = n_zl * LANES
    per = n_union // n_zl
    shape = jax.ShapeDtypeStruct
    ids = union_ids.reshape(1, n_union)
    gain = norm_gain.reshape(1, width)
    at_y, at_x, at_core, at_zl = (v.reshape(1) for v in (y, x, core, zl))

    inputs = (hidden_in, key_cotangent, value_cotangent, ids, gain)
    packed = pl.pallas_call(
        prepare,
        out_shape=shape((n_x, n_zl, toks + per + AUX, LANES), bf16),
        in_specs=[SMEM] + [pl.BlockSpec(memory_space=pl.ANY)] * len(inputs),
        out_specs=VMEM,
        scratch_shapes=[pltpu.VMEM(v.shape, v.dtype) for v in inputs]
        + [pltpu.SemaphoreType.DMA((len(inputs),))],
        compiler_params=pltpu.CompilerParams(vmem_limit_bytes=60 * 1024 * 1024),
    )(at_zl, *inputs)
    packed = exchange(packed.reshape((n_x * n_zl,) + packed.shape[2:]), ("x", "zl"))
    few = per // (n_y * n_core)
    right, scale, outliers = call(
        lambda *refs: unpack(float(width * n_zl), *refs),
        (
            shape((n_x, toks, cols), bf16),
            shape((AUX, n_x * LANES), f32),
            shape((n_y * n_core, few, cols), f32),
        ),
        (at_zl, packed.reshape((n_x, n_zl) + packed.shape[1:])),
        1,
        [pltpu.VMEM((LANES, LANES), f32)],
    )
    left = [hidden_in] + [shift(hidden_in, "x", k) for k in range(1, n_x)]

    outliers = exchange(outliers, ("y", "core"))
    outliers = call(
        lambda *refs: sum_spread(n_y * n_core, *refs),
        shape((n_zh * n_zl, few, cols), bf16),
        (outliers,),
    )
    outliers = exchange(outliers, ("zl", "zh"))
    outliers = call(
        lambda *refs: sum_last(n_zh, *refs),
        shape((1, n_zl * few, cols), bf16),
        (outliers,),
    )

    half = shape((n_y, width // (n_y * n_core), cols), f32)
    anywhere = pl.BlockSpec(memory_space=pl.ANY)
    own, other = pl.pallas_call(
        multiply,
        out_shape=(half, shape(half.shape, bf16)),
        in_specs=[SMEM, SMEM] + [anywhere] * (3 + n_x),
        out_specs=(anywhere, anywhere),
        scratch_shapes=[
            pltpu.VMEM(gain.shape, f32),
            pltpu.VMEM(scale.shape, f32),
            pltpu.VMEM(right.shape, bf16),
            pltpu.VMEM((n_x, toks, width), bf16),
            pltpu.VMEM((2, width // n_y, cols), f32),
            pltpu.VMEM((2, width // (n_y * n_core), cols), bf16),
            pltpu.SemaphoreType.DMA((n_y + 1, n_x)),
            pltpu.SemaphoreType.DMA((2, 2)),
        ],
        cost_estimate=pl.CostEstimate(flops=0, bytes_accessed=128 * 1024 * 1024, transcendentals=0),
        compiler_params=pltpu.CompilerParams(vmem_limit_bytes=60 * 1024 * 1024),
    )(at_x, at_core, gain, scale, right, *left)
    other, outliers = lax.optimization_barrier((other, outliers))
    got = shift(other, "core", 1)
    own = pl.pallas_call(
        fetch,
        out_shape=half,
        in_specs=[anywhere],
        out_specs=VMEM,
        scratch_shapes=[pltpu.SemaphoreType.DMA((n_y,))],
        cost_estimate=pl.CostEstimate(flops=0, bytes_accessed=16 * 1024 * 1024, transcendentals=0),
        compiler_params=PARAMS,
    )(own)
    rows = width // (n_y * n_core * n_x * n_zh)
    lines = n_zh * rows + n_zl * few
    pieces = call(add_cores, shape((n_y, n_x, lines, cols), bf16), (own, got, outliers))
    pieces = exchange(pieces.reshape(n_y * n_x, lines, cols), ("y", "x"))
    pieces, outliers = call(
        add_y,
        (shape((n_zh, n_x, rows, cols), bf16), shape((n_y, n_x, n_zl * few, cols), bf16)),
        (pieces.reshape(n_y, n_x, lines, cols),),
    )
    union = shape((n_union, heads), f32)
    union_key, union_value = call(
        lambda *refs: lay_out(n_zl, *refs),
        (union, union),
        (at_core, outliers, shift(outliers, "core", 1)),
        1,
    )
    pieces = exchange(pieces, "zh")
    first = zl * width + rows * (((y * n_core + core) * n_x + x) * n_zh + zh)
    grad = shape((1, rows, heads), f32)
    grad_key, grad_value = call(finish, (grad, grad), (first.reshape(1), ids, pieces), 1)
    return (grad_key, grad_value, union_key, union_value)


def solution(mesh):
    sizes = dict(mesh.shape)
    split = Mesh(
        mesh.devices.reshape(sizes["group"] // 2, 2, 4, sizes["loop"] // 4, sizes["mp"]), AXES
    )
    rows = ("y", "core", "x", "zh")
    return jax.shard_map(
        per_device,
        mesh=split,
        in_specs=(P(rows, "zl"), P("zl"), P(rows, "zl"), P(rows, "zl"), P()),
        out_specs=(P("zl", rows, None), P("zl", rows, None), P(), P()),
        check_vma=False,
    )
```

```python
import jax
import jax.numpy as jnp
from jax import lax
from jax.experimental import pallas as pl
from jax.experimental.pallas import tpu as pltpu
from jax.sharding import Mesh, PartitionSpec as P

AXES = ("y", "core", "x", "zh", "zl")
LANES = 128
AUX = 8
VMEM = pl.BlockSpec(memory_space=pltpu.VMEM)
SMEM = pl.BlockSpec(memory_space=pltpu.SMEM)
PARAMS = pltpu.CompilerParams(vmem_limit_bytes=20 * 1024 * 1024)


def split3(v):
    hi = v.astype(jnp.bfloat16).astype(jnp.float32)
    mid = (v - hi).astype(jnp.bfloat16).astype(jnp.float32)
    low = (v - hi - mid).astype(jnp.bfloat16).astype(jnp.float32)
    return hi, mid, low


def column(row):
    return jnp.broadcast_to(row, (LANES, LANES)).T


def prepare(zl_ref, hidden_in, key_in, value_in, ids_in, gain_in, *refs):
    packed_ref, hidden_ref, key_ref, value_ref, ids_ref, gain_ref, sems = refs
    copies = [
        pltpu.make_async_copy(source, target, sems.at[i])
        for i, (source, target) in enumerate(
            [
                (hidden_in, hidden_ref),
                (key_in, key_ref),
                (value_in, value_ref),
                (ids_in, ids_ref),
                (gain_in, gain_ref),
            ]
        )
    ]
    for copy in copies:
        copy.start()
    n_x, n_zl, _, _ = packed_ref.shape
    toks, width = hidden_ref.shape
    n_union = ids_ref.shape[1]
    per = n_union // n_zl
    for copy in copies[1:]:
        copy.wait()
    for x in range(n_x):
        source = key_ref if x < n_x // 2 else value_ref
        at = LANES * (x % (n_x // 2))
        for z in range(n_zl):
            packed_ref[x, z, :toks] = source[:, at : at + LANES]
    ids = column(ids_ref[...].astype(jnp.float32))[:, :1].astype(jnp.int32) - zl_ref[0] * width
    hit = lax.broadcasted_iota(jnp.int32, (n_union, width), 1) == ids
    gains = jnp.sum(jnp.where(hit, gain_ref[...], 0.0), axis=1, keepdims=True)
    copies[0].wait()
    hidden = hidden_ref[...]
    both = lax.dot_general(
        jnp.concatenate([jnp.where(hit, 1.0, 0.0).astype(jnp.bfloat16), hidden], axis=0),
        hidden,
        (((1,), (1,)), ((), ())),
        preferred_element_type=jnp.float32,
    )
    picked = both[:n_union].astype(jnp.bfloat16)
    row = lax.broadcasted_iota(jnp.int32, (toks, LANES), 0)
    lane = lax.broadcasted_iota(jnp.int32, (toks, LANES), 1)
    squares = jnp.sum(jnp.where(row == lane, both[n_union:], 0.0), axis=0, keepdims=True)
    gains = jnp.broadcast_to(gains, (n_union, LANES)).T[:1]
    table = jnp.zeros((AUX, LANES), jnp.float32)
    for place, part in enumerate(split3(squares) + split3(gains)):
        table = jnp.where(row[:AUX] == place, part, table)
    extra = table.astype(jnp.bfloat16)
    for x in range(n_x):
        for z in range(n_zl):
            packed_ref[x, z, toks : toks + per] = picked[per * z : per * (z + 1)]
            packed_ref[x, z, toks + per :] = extra


def unpack(features, zl_ref, in_ref, out_ref, scale_ref, union_ref, gain_ref):
    n_x, n_zl, rows, _ = in_ref.shape
    toks = LANES
    per = rows - toks - AUX
    total = jnp.zeros((per, n_zl * LANES), jnp.float32)
    for x in range(n_x):
        extra = in_ref[x, 0, toks + per :].astype(jnp.float32)
        picked = in_ref[x, 0, toks : toks + per].astype(jnp.float32)
        for z in range(1, n_zl):
            extra = extra + in_ref[x, z, toks + per :].astype(jnp.float32)
            picked = picked + in_ref[x, z, toks : toks + per].astype(jnp.float32)
        if x == 0:
            gain_ref[...] = column(extra[3:4] + extra[4:5] + extra[5:6])
        squares = extra[0:1] + extra[1:2] + extra[2:3]
        scale = lax.rsqrt(squares / features + 1e-05)
        gains = gain_ref[pl.ds(pl.multiple_of(zl_ref[0] * per, per), per), :]
        normed = (picked * scale * gains).astype(jnp.bfloat16)
        right = jnp.concatenate([in_ref[x, z, :toks] for z in range(n_zl)], axis=1)
        total = total + jnp.dot(normed, right, preferred_element_type=jnp.float32)
        out_ref[x] = right
        table = jnp.zeros((AUX, LANES), jnp.float32) + scale
        scale_ref[:, x * LANES : (x + 1) * LANES] = table
    count, few, _ = union_ref.shape
    for i in range(count):
        union_ref[i] = total[i * few : (i + 1) * few].astype(union_ref.dtype)


def sum_spread(groups, in_ref, out_ref):
    count = in_ref.shape[0]
    rest = count // groups
    few = in_ref.shape[1]
    for j in range(rest):
        total = in_ref[j].astype(jnp.float32)
        for i in range(1, groups):
            total = total + in_ref[i * rest + j].astype(jnp.float32)
        total = total.astype(jnp.bfloat16)
        for to in range(out_ref.shape[0]):
            out_ref[to, j * few : (j + 1) * few] = total


def multiply(x_ref, core_ref, gain_in, scale_in, right_in, *refs):
    lefts, refs = refs[:-10], refs[-10:]
    own_out, other_out, gain_ref, scale_ref, right_ref, left_ref, total_ref, half_ref, in_sems, out_sems = refs
    n_x, n_y = len(lefts), own_out.shape[0]
    toks, width = lefts[0].shape
    tile = width // n_y
    pairs = [(gain_in, gain_ref), (scale_in, scale_ref), (right_in, right_ref)]
    copies = [pltpu.make_async_copy(a, b, in_sems.at[n_y, i]) for i, (a, b) in enumerate(pairs)]
    quarters = []
    for y in range(n_y):
        at = pl.ds(y * tile, tile)
        quarters.append(
            [
                pltpu.make_async_copy(left.at[:, at], left_ref.at[j, :, at], in_sems.at[y, j])
                for j, left in enumerate(lefts)
            ]
        )
    for copy in copies + sum(quarters, []):
        copy.start()
    for copy in copies:
        copy.wait()
    columns, right = [], []
    for j in range(n_x):
        x = lax.rem(x_ref[0] + n_x - j, n_x)
        row = scale_ref[:1, pl.ds(pl.multiple_of(x * LANES, LANES), LANES)]
        columns.append(jnp.concatenate([column(row)] * (tile // LANES), axis=1))
        right.append(right_ref[x])
    right = jnp.concatenate(right, axis=0)
    rows = tile // 2
    own_rows = pl.ds(pl.multiple_of(core_ref[0] * rows, rows), rows)
    other_rows = pl.ds(pl.multiple_of((1 - core_ref[0]) * rows, rows), rows)
    sent = []
    for y in range(n_y):
        at, slot = slice(y * tile, (y + 1) * tile), y % 2
        for copy in quarters[y]:
            copy.wait()
        normed = []
        for j in range(n_x):
            left = left_ref[j, :, at].astype(jnp.float32) * columns[j] * gain_ref[:, at]
            normed.append(left.astype(jnp.bfloat16))
        if y >= 2:
            for copy in sent[y - 2]:
                copy.wait()
        total_ref[slot] = lax.dot_general(
            jnp.concatenate(normed, axis=0),
            right,
            (((0,), (0,)), ((), ())),
            preferred_element_type=jnp.float32,
        )
        half_ref[slot] = total_ref[slot, other_rows, :].astype(jnp.bfloat16)
        sent.append(
            (
                pltpu.make_async_copy(total_ref.at[slot, own_rows], own_out.at[y], out_sems.at[slot, 0]),
                pltpu.make_async_copy(half_ref.at[slot], other_out.at[y], out_sems.at[slot, 1]),
            )
        )
        for copy in sent[y]:
            copy.start()
    for pair in sent[-2:]:
        for copy in pair:
            copy.wait()


def fetch(source, out_ref, sems):
    count = out_ref.shape[0]
    copies = [pltpu.make_async_copy(source.at[y], out_ref.at[y], sems.at[y]) for y in range(count)]
    for copy in copies:
        copy.start()
    for copy in copies:
        copy.wait()


def add_cores(own_ref, got_ref, union_ref, out_ref):
    n_y, n_x, rows, _ = out_ref.shape
    rows -= union_ref.shape[1]
    for y in range(n_y):
        for x in range(n_x):
            at = slice(x * rows, (x + 1) * rows)
            out_ref[y, x, :rows] = (own_ref[y, at] + got_ref[y, at].astype(jnp.float32)).astype(jnp.bfloat16)
            out_ref[y, x, rows:] = union_ref[0]


def add_y(in_ref, out_ref, union_ref):
    n_y, n_x, _, _ = in_ref.shape
    n_zh, _, rows, _ = out_ref.shape
    for x in range(n_x):
        for z in range(n_zh):
            at = slice(z * rows, (z + 1) * rows)
            total = in_ref[0, x, at].astype(jnp.float32)
            for y in range(1, n_y):
                total = total + in_ref[y, x, at].astype(jnp.float32)
            out_ref[z, x] = total.astype(jnp.bfloat16)
        for y in range(n_y):
            union_ref[y, x] = in_ref[y, x, n_zh * rows :]


def finish(first_ref, ids_ref, in_ref, key_ref, value_ref):
    n_zh, n_x, rows, cols = in_ref.shape
    row = lax.broadcasted_iota(jnp.int32, (rows, LANES), 0) + first_ref[0]
    hits = jnp.sum(jnp.where(row == ids_ref[...], 1.0, 0.0), axis=1, keepdims=True)
    for x in range(n_x):
        total = in_ref[0, x].astype(jnp.float32)
        for z in range(1, n_zh):
            total = total + in_ref[z, x].astype(jnp.float32)
        total = jnp.where(hits > 0.0, 0.0, total)
        out_ref = value_ref if x // 2 else key_ref
        for z in range(cols // LANES):
            at = LANES * (2 * z + x % 2)
            out_ref[0, :, at : at + LANES] = total[:, z * LANES : (z + 1) * LANES]


def lay_out(n_zl, core_ref, own_ref, got_ref, key_ref, value_ref):
    n_y, n_x, rows, cols = own_ref.shape
    few = rows // n_zl
    per = key_ref.shape[0] // n_zl
    first = core_ref[0] == 0
    for x in range(n_x):
        out_ref = value_ref if x // 2 else key_ref
        blocks = []
        for y in range(n_y):
            own, got = own_ref[y, x].astype(jnp.float32), got_ref[y, x].astype(jnp.float32)
            blocks += [jnp.where(first, own, got), jnp.where(first, got, own)]
        for z in range(n_zl):
            lines = jnp.concatenate([block[few * z : few * (z + 1)] for block in blocks], axis=0)
            for j in range(cols // LANES):
                at = LANES * (2 * j + x % 2)
                out_ref[per * z : per * (z + 1), at : at + LANES] = lines[:, j * LANES : (j + 1) * LANES]


def call(body, out_shape, args, scalars=0, scratch=(), cost=0):
    single = not isinstance(out_shape, tuple)
    return pl.pallas_call(
        body,
        out_shape=out_shape,
        in_specs=[SMEM] * scalars + [VMEM] * (len(args) - scalars),
        out_specs=VMEM if single else tuple(VMEM for _ in out_shape),
        scratch_shapes=scratch,
        cost_estimate=pl.CostEstimate(flops=0, bytes_accessed=cost, transcendentals=0) if cost else None,
        compiler_params=PARAMS,
    )(*args)


def exchange(v, axes):
    return lax.all_to_all(v, axes, split_axis=0, concat_axis=0, tiled=True)


def shift(v, axis, by):
    count = lax.axis_size(axis)
    return lax.ppermute(v, axis, [(i, (i + by) % count) for i in range(count)])


def per_device(hidden_in, norm_gain, key_cotangent, value_cotangent, union_ids):
    bf16, f32 = jnp.bfloat16, jnp.float32
    toks, width = hidden_in.shape
    n_y, n_core, n_x, n_zh, n_zl = (lax.axis_size(a) for a in AXES)
    y, core, x, zh, zl = (lax.axis_index(a).astype(jnp.int32) for a in AXES)
    n_union = union_ids.shape[0]
    heads = key_cotangent.shape[1] * n_zl
    cols = n_zl * LANES
    per = n_union // n_zl
    shape = jax.ShapeDtypeStruct
    ids = union_ids.reshape(1, n_union)
    gain = norm_gain.reshape(1, width)
    at_y, at_x, at_core, at_zl = (v.reshape(1) for v in (y, x, core, zl))

    inputs = (hidden_in, key_cotangent, value_cotangent, ids, gain)
    packed = pl.pallas_call(
        prepare,
        out_shape=shape((n_x, n_zl, toks + per + AUX, LANES), bf16),
        in_specs=[SMEM] + [pl.BlockSpec(memory_space=pl.ANY)] * len(inputs),
        out_specs=VMEM,
        scratch_shapes=[pltpu.VMEM(v.shape, v.dtype) for v in inputs]
        + [pltpu.SemaphoreType.DMA((len(inputs),))],
        compiler_params=pltpu.CompilerParams(vmem_limit_bytes=60 * 1024 * 1024),
    )(at_zl, *inputs)
    packed = exchange(packed.reshape((n_x * n_zl,) + packed.shape[2:]), ("x", "zl"))
    few = per // (n_y * n_core)
    right, scale, outliers = call(
        lambda *refs: unpack(float(width * n_zl), *refs),
        (
            shape((n_x, toks, cols), bf16),
            shape((AUX, n_x * LANES), f32),
            shape((n_y * n_core, few, cols), bf16),
        ),
        (at_zl, packed.reshape((n_x, n_zl) + packed.shape[1:])),
        1,
        [pltpu.VMEM((LANES, LANES), f32)],
    )
    left = [hidden_in] + [shift(hidden_in, "x", k) for k in range(1, n_x)]

    outliers = exchange(outliers, ("y", "core"))
    outliers = call(
        lambda *refs: sum_spread(n_y * n_core, *refs),
        shape((n_zh * n_zl, few, cols), bf16),
        (outliers,),
    )
    outliers = exchange(outliers, ("zh", "zl"))
    outliers = call(
        lambda *refs: sum_spread(n_zh, *refs),
        shape((1, n_zl * few, cols), bf16),
        (outliers,),
    )

    half = shape((n_y, width // (n_y * n_core), cols), f32)
    anywhere = pl.BlockSpec(memory_space=pl.ANY)
    own, other = pl.pallas_call(
        multiply,
        out_shape=(half, shape(half.shape, bf16)),
        in_specs=[SMEM, SMEM] + [anywhere] * (3 + n_x),
        out_specs=(anywhere, anywhere),
        scratch_shapes=[
            pltpu.VMEM(gain.shape, f32),
            pltpu.VMEM(scale.shape, f32),
            pltpu.VMEM(right.shape, bf16),
            pltpu.VMEM((n_x, toks, width), bf16),
            pltpu.VMEM((2, width // n_y, cols), f32),
            pltpu.VMEM((2, width // (n_y * n_core), cols), bf16),
            pltpu.SemaphoreType.DMA((n_y + 1, n_x)),
            pltpu.SemaphoreType.DMA((2, 2)),
        ],
        cost_estimate=pl.CostEstimate(flops=0, bytes_accessed=128 * 1024 * 1024, transcendentals=0),
        compiler_params=pltpu.CompilerParams(vmem_limit_bytes=60 * 1024 * 1024),
    )(at_x, at_core, gain, scale, right, *left)
    other, outliers = lax.optimization_barrier((other, outliers))
    got = shift(other, "core", 1)
    own = pl.pallas_call(
        fetch,
        out_shape=half,
        in_specs=[anywhere],
        out_specs=VMEM,
        scratch_shapes=[pltpu.SemaphoreType.DMA((n_y,))],
        cost_estimate=pl.CostEstimate(flops=0, bytes_accessed=16 * 1024 * 1024, transcendentals=0),
        compiler_params=PARAMS,
    )(own)
    rows = width // (n_y * n_core * n_x * n_zh)
    lines = n_zh * rows + n_zl * few
    pieces = call(add_cores, shape((n_y, n_x, lines, cols), bf16), (own, got, outliers))
    pieces = exchange(pieces.reshape(n_y * n_x, lines, cols), ("y", "x"))
    pieces, outliers = call(
        add_y,
        (shape((n_zh, n_x, rows, cols), bf16), shape((n_y, n_x, n_zl * few, cols), bf16)),
        (pieces.reshape(n_y, n_x, lines, cols),),
    )
    union = shape((n_union, heads), f32)
    union_key, union_value = call(
        lambda *refs: lay_out(n_zl, *refs),
        (union, union),
        (at_core, outliers, shift(outliers, "core", 1)),
        1,
    )
    pieces = exchange(pieces, "zh")
    first = zl * width + rows * (((y * n_core + core) * n_x + x) * n_zh + zh)
    grad = shape((1, rows, heads), f32)
    grad_key, grad_value = call(finish, (grad, grad), (first.reshape(1), ids, pieces), 1)
    return (grad_key, grad_value, union_key, union_value)


def solution(mesh):
    sizes = dict(mesh.shape)
    split = Mesh(
        mesh.devices.reshape(sizes["group"] // 2, 2, 4, sizes["loop"] // 4, sizes["mp"]), AXES
    )
    rows = ("y", "core", "x", "zh")
    return jax.shard_map(
        per_device,
        mesh=split,
        in_specs=(P(rows, "zl"), P("zl"), P(rows, "zl"), P(rows, "zl"), P()),
        out_specs=(P("zl", rows, None), P("zl", rows, None), P(), P()),
        check_vma=False,
    )
```
